512 devices in a mesh: row: 16 (over x, y_hi), col: 16 (over z, core), depth: 2 (over y_lo).
Axes of the slice: x: 4, y: 8 (y_hi: 4, y_lo: 2; y = y_hi * 2 + y_lo), z: 8, core: 2. Of those that a mesh axis runs over, the one named last changes fastest.
Arguments:
- embeddings: bfloat16 [64, 32768], P(None, ('row', 'col', 'depth')), may hold values from -6 to 6
- coords: float32 [16, 32768], P(None, ('row', 'col', 'depth')), may hold values from -4 to 4
- pair_weight: bfloat16 [32768, 32768], P('row', ('col', 'depth')), may hold values from 0.0125 to 28.8, as said below
Outputs:
- new_coords: float32 [16, 32768], P(None, ('row', 'col', 'depth'))
- stress: float32 [], replicated
The draws below stay inside these ranges and needn't reach their ends.
Inputs may be any that keep to these rules, and one draw needn't show every extreme that they name: `pair_weight`: every weight is positive.
All inputs are finite; a program needn't handle non-finite values.
Results may differ from the reference program's by a relative error of at most 0.00035.
Values may be sent and summed in bfloat16 or wider, within the bound.
No kernel may reach another device: no remote copies, remote signals or barrier semaphores. Data moves between devices by JAX's collectives and lax.ppermute only.
A program may use at most 64 MiB of HBM per device.

```python
import jax
import jax.numpy as jnp
from jax import lax

FEAT = 64
DIM = 16
POINTS = 32768


def draw_pair_weight(key, part):
    key = jax.random.fold_in(key, 11)
    k_rows, k_cols, k_each = jax.random.split(key, 3)
    top = 10.0
    low = 0.5
    high = 1.5
    row_scale = jnp.exp(jax.random.uniform(k_rows, (POINTS, 1), jnp.float32) * jnp.log(top))
    col_scale = jnp.exp(jax.random.uniform(k_cols, (1, POINTS), jnp.float32) * jnp.log(top))
    jitter = jax.random.uniform(k_each, (POINTS, POINTS), jnp.float32, minval=low, maxval=high)
    return (row_scale * col_scale * jitter / top).astype(jnp.bfloat16)


def steps_of(key, extent, cuts, smallest, high):
    level = 1.0
    for axis_at, blocks in cuts:
        steps = jax.random.uniform(jax.random.fold_in(jax.random.fold_in(key, 6), axis_at), (blocks,), jnp.float32, smallest / len(cuts), high / len(cuts))
        level = level * jnp.repeat(jnp.exp(steps), extent[axis_at] // blocks).reshape((-1,) + (1,) * (len(extent) - 1 - axis_at))
    return level


def scatter_about(own_key, extent, spread, most, cuts=(), kind=jnp.bfloat16):
    gain = steps_of(own_key, extent, cuts, -0.22, 0.18) if cuts else 1.0
    result = jax.random.normal(own_key, extent, jnp.float32) * spread * gain
    return jnp.minimum(jnp.maximum(result, -most), most).astype(kind)


def setup_inputs(seed: int = 0) -> dict:
    arg_keys = jax.random.split(jax.random.key(seed), 4)
    embeddings = scatter_about(arg_keys[0], (FEAT, POINTS), 1.0, 6.0, ((1, 512),))
    coords = scatter_about(arg_keys[1], (DIM, POINTS), 0.5, 4.0, ((1, 512),), jnp.float32)
    pair_weight = draw_pair_weight(jax.random.fold_in(arg_keys[3], 71), 0)
    return dict(embeddings=embeddings, coords=coords, pair_weight=pair_weight)


def reference(embeddings, coords, pair_weight):
    hi = lax.Precision.HIGHEST
    feats = embeddings.astype(jnp.float32)
    feat_sq = lax.optimization_barrier(jnp.sum(feats * feats, axis=0))
    crd_sq = lax.optimization_barrier(jnp.sum(coords * coords, axis=0))
    total = coords.shape[1]
    blk = min(512, total)
    starts = jnp.arange(0, total, blk).astype(jnp.int32)

    def one_block(start):
        f_rows = lax.dynamic_slice_in_dim(feats, start, blk, 1)
        x_rows = lax.dynamic_slice_in_dim(coords, start, blk, 1)
        fs_rows = lax.dynamic_slice_in_dim(feat_sq, start, blk, 0)
        xs_rows = lax.dynamic_slice_in_dim(crd_sq, start, blk, 0)
        weights = lax.dynamic_slice_in_dim(pair_weight, start, blk, 0).astype(jnp.float32)
        gram_f = lax.dot_general(f_rows, feats, (((0,), (0,)), ((), ())), precision=hi, preferred_element_type=jnp.float32)
        dissim = jnp.sqrt(jnp.maximum(fs_rows[:, None] + feat_sq[None, :] - 2.0 * gram_f, 0.0)) / 8.0
        gram_x = lax.dot_general(x_rows, coords, (((0,), (0,)), ((), ())), precision=hi, preferred_element_type=jnp.float32)
        dist = jnp.sqrt(jnp.maximum(xs_rows[:, None] + crd_sq[None, :] - 2.0 * gram_x, 0.0))
        cmat = weights * dissim / jnp.maximum(dist, 1.0) - weights
        pull = lax.dot_general(coords, cmat, (((1,), (1,)), ((), ())), precision=hi, preferred_element_type=jnp.float32)
        rate = lax.optimization_barrier(jnp.sum(cmat, axis=1))
        wsum = lax.optimization_barrier(jnp.sum(weights, axis=1))
        misfit = lax.optimization_barrier(jnp.sum(weights * (dissim - dist) ** 2, axis=1))
        scale = lax.optimization_barrier(jnp.sum(weights * dissim * dissim, axis=1))
        return jnp.concatenate([pull, jnp.stack([rate, wsum, misfit, scale], axis=0)], axis=0)
    parts = lax.map(one_block, starts)
    sums = jnp.transpose(parts, (1, 0, 2)).reshape(parts.shape[1], total)
    dims = coords.shape[0]
    pull = sums[:dims]
    rate = sums[dims]
    wsum = sums[dims + 1]
    new_coords = coords + (rate[None, :] * coords - pull) / wsum[None, :]
    stress = jnp.sum(sums[dims + 2]) / jnp.sum(sums[dims + 3])
    return (new_coords, stress)
```

```python
import jax
import jax.numpy as jnp
from jax import lax
from jax.experimental import pallas as pl
from jax.experimental.pallas import tpu as pltpu
from jax.sharding import PartitionSpec as P

F32 = jnp.float32
BF16 = jnp.bfloat16

EMB, XH, XL, XH2, QF, QX, ONE, LANES = 0, 64, 80, 96, 112, 115, 118, 128
TINY = 1e-30


def bilinear_form(kind):
    a = lax.broadcasted_iota(jnp.int32, (LANES, LANES), 0)
    b = lax.broadcasted_iota(jnp.int32, (LANES, LANES), 1)

    def band(first, count, shift):
        return (a >= first) & (a < first + count) & (b == a + shift)

    if kind == 0:
        cross = band(EMB, 64, 0)
        square, unit = QF, 1.0 / 64.0
    else:
        cross = band(XH, 16, 0) | band(XL, 16, XH2 - XL) | band(XH2, 16, XL - XH2)
        square, unit = QX, 1.0
    norms = band(square, 3, ONE - square) | band(ONE, 3, square - ONE)
    return jnp.where(cross, -2.0 * unit, jnp.where(norms, unit, 0.0)).astype(BF16)


def split3(value):
    hi = value.astype(BF16).astype(F32)
    mid = (value - hi).astype(BF16).astype(F32)
    low = (value - hi - mid).astype(BF16).astype(F32)
    return hi, mid, low


def pack_kernel(emb_ref, crd_ref, own_ref, out_ref):
    emb = emb_ref[...].astype(F32)
    crd = crd_ref[...]
    points = emb.shape[1]
    hi = crd.astype(BF16).astype(F32)
    low = (crd - hi).astype(BF16).astype(F32)
    squares = split3(jnp.sum(emb * emb, axis=0, keepdims=True))
    squares += split3(jnp.sum(crd * crd, axis=0, keepdims=True))
    lane = lax.broadcasted_iota(jnp.int32, (16, points), 0)
    tail = jnp.where((lane >= ONE - QF) & (lane < ONE - QF + 3), 1.0, 0.0)
    for k, sq in enumerate(squares):
        tail = jnp.where(lane == k, sq, tail)
    rows = jnp.concatenate([emb, hi, low, hi, tail], axis=0)
    mine = rows.T.astype(BF16)
    own_ref[...] = mine
    for k in range(out_ref.shape[0]):
        out_ref[k] = mine


def pairs_kernel(row_ref, col_ref, w_hbm, out_ref, w_ref, f_scr, x_scr, sems):
    total_rows = row_ref.shape[0]
    total = col_ref.shape[0]
    tm = min(256, total_rows)
    tn = min(256, total)
    per = tm // 64
    steps = total_rows // tm

    def fetch(i):
        at = pl.ds(i * tm, tm)
        return pltpu.make_async_copy(w_hbm.at[at, :], w_ref.at[at, :], sems.at[i])

    for i in range(steps):
        fetch(i).start()
    all_cols = col_ref[...]
    dims = (((1,), (1,)), ((), ()))
    form_f = bilinear_form(0)
    f_scr[...] = lax.dot_general(form_f, all_cols, dims, preferred_element_type=F32).astype(BF16)
    x_scr[...] = lax.dot_general(bilinear_form(1), all_cols, dims, preferred_element_type=F32).astype(BF16)
    lane = lax.broadcasted_iota(jnp.int32, (tm, LANES), 1)

    def block(i, carry):
        mis, scl = carry
        fetch(i).wait()
        at = pl.ds(pl.multiple_of(i * tm, tm), tm)
        rows = row_ref[at, :]
        acc = jnp.zeros((tm, LANES), F32)
        wacc = jnp.zeros((tm, LANES), F32)
        for start in range(0, total, tn):
            cut = slice(start, start + tn)
            f2 = jnp.dot(rows, f_scr[:, cut], preferred_element_type=F32)
            x2 = jnp.dot(rows, x_scr[:, cut], preferred_element_type=F32)
            wb = w_ref[at, cut]
            w = wb.astype(F32)
            f2 = jnp.maximum(f2, TINY)
            x2 = jnp.maximum(x2, TINY)
            dissim = f2 * lax.rsqrt(f2)
            inv = lax.rsqrt(x2)
            diff = dissim - x2 * inv
            cmat = w * (dissim * jnp.minimum(inv, 1.0) - 1.0)
            mis += jnp.sum((w * (diff * diff)).reshape(tm // 8, 8, tn), axis=0)
            cols = col_ref[cut, :]
            acc += jnp.dot(cmat.astype(BF16), cols, preferred_element_type=F32)
            wacc += jnp.dot(wb, cols, preferred_element_type=F32)
        bent = jnp.dot(rows, form_f, preferred_element_type=F32)
        scl += jnp.sum((bent * wacc).reshape(tm // 8, 8, LANES), axis=0)
        sums = jnp.where(lane == ONE + 1, wacc, acc).T
        pull = sums[XH : XH + 16] + sums[XL : XL + 16]
        rate = sums[ONE : ONE + 1]
        wsum = sums[ONE + 1 : ONE + 2]
        for k in range(per):
            cut = slice(64 * k, 64 * k + 64)
            out_ref[i * per + k, 0:8, :] = jnp.concatenate([pull[0:8, cut], pull[8:16, cut]], axis=1)
            out_ref[i * per + k, 8:9, :] = jnp.concatenate([rate[:, cut], wsum[:, cut]], axis=1)
        return mis, scl

    mis, scl = lax.fori_loop(
        0, steps, block, (jnp.zeros((8, tn), F32), jnp.zeros((8, LANES), F32))
    )
    mis = jnp.sum(mis, axis=0, keepdims=True)
    mis = sum(mis[:, k : k + 128] for k in range(0, tn, 128))
    scl = jnp.sum(scl, axis=0, keepdims=True)
    count = out_ref.shape[0]
    out_ref[:, 9:10, :] = jnp.broadcast_to(mis[None], (count, 1, 128))
    out_ref[:, 10:11, :] = jnp.broadcast_to(scl[None], (count, 1, 128))
    out_ref[:, 11:16, :] = jnp.zeros((count, 5, 128), F32)


def finish_kernel(part_ref, crd_ref, new_ref, share_ref):
    sums = jnp.sum(part_ref[...], axis=0)
    rate = sums[8:9, 0:64]
    wsum = sums[8:9, 64:128]
    pull = jnp.concatenate([sums[0:8, 0:64], sums[0:8, 64:128]], axis=0)
    crd = crd_ref[...]
    new_ref[...] = crd + (rate * crd - pull) / wsum
    share_ref[...] = jnp.broadcast_to(sums[8:16][None], share_ref.shape)


def stress_kernel(part_ref, out_ref):
    sums = jnp.sum(part_ref[...], axis=0)
    out_ref[...] = jnp.sum(sums[1:2], axis=1, keepdims=True) / jnp.sum(sums[2:3], axis=1, keepdims=True)


def column_moves(n_row, n_col, n_depth):
    moves = []
    for row in range(n_row):
        for at in range(n_col * n_depth):
            moves.append((row * n_col * n_depth + at, (at % n_row * n_col + row) * n_depth + at // n_row))
    return moves


def shards(embeddings, coords, pair_weight):
    rows, cols = pair_weight.shape
    points = embeddings.shape[1]
    group = rows // points
    n_row, n_col, n_depth = (lax.axis_size(a) for a in ("row", "col", "depth"))

    packed = pl.pallas_call(
        pack_kernel,
        out_shape=(
            jax.ShapeDtypeStruct((points, LANES), BF16),
            jax.ShapeDtypeStruct((group, points, LANES), BF16),
        ),
        name="pack",
    )(embeddings, coords)
    moved = lax.ppermute(packed[0], ("row", "col", "depth"), column_moves(n_row, n_col, n_depth))
    t_rows = lax.all_to_all(packed[1], ("col", "depth"), 0, 0, tiled=True).reshape(rows, LANES)
    moved = jnp.broadcast_to(moved[None], (n_row, points, LANES))
    t_cols = lax.all_to_all(moved, "row", 0, 0, tiled=True).reshape(cols, LANES)

    vmem = pl.BlockSpec(memory_space=pltpu.VMEM)
    parts = pl.pallas_call(
        pairs_kernel,
        in_specs=[vmem, vmem, pl.BlockSpec(memory_space=pltpu.HBM)],
        out_specs=vmem,
        out_shape=jax.ShapeDtypeStruct((group, 16, 128), F32),
        scratch_shapes=[
            pltpu.VMEM((rows, cols), BF16),
            pltpu.VMEM((LANES, cols), BF16),
            pltpu.VMEM((LANES, cols), BF16),
            pltpu.SemaphoreType.DMA((max(1, rows // 256),)),
        ],
        compiler_params=pltpu.CompilerParams(vmem_limit_bytes=60 * 1024 * 1024),
        name="pairs",
    )(t_rows, t_cols, pair_weight)
    parts = lax.all_to_all(parts, ("col", "depth"), 0, 0, tiled=True)
    new_coords, shares = pl.pallas_call(
        finish_kernel,
        out_shape=(
            jax.ShapeDtypeStruct(coords.shape, F32),
            jax.ShapeDtypeStruct((n_row, 8, 128), F32),
        ),
        name="finish",
    )(parts, coords)
    shares = lax.all_to_all(shares, "row", 0, 0, tiled=True)
    stress = pl.pallas_call(
        stress_kernel,
        out_shape=jax.ShapeDtypeStruct((1, 1), F32),
        name="stress",
    )(shares)
    return (new_coords, stress[0, 0])


def solution(mesh):
    placed = (
        P(None, ("row", "col", "depth")),
        P(None, ("row", "col", "depth")),
        P("row", ("col", "depth")),
    )
    return jax.shard_map(
        shards,
        mesh=mesh,
        in_specs=placed,
        out_specs=(P(None, ("row", "col", "depth")), P()),
        check_vma=False,
    )
```

```python
import jax
import jax.numpy as jnp
from jax import lax
from jax.experimental import pallas as pl
from jax.experimental.pallas import tpu as pltpu
from jax.sharding import PartitionSpec as P

F32 = jnp.float32
BF16 = jnp.bfloat16

EMB, XH, XL, XH2, QF, QX, ONE, LANES = 0, 64, 80, 96, 112, 115, 118, 128
TINY = 1e-30


def bilinear_form(kind):
    a = lax.broadcasted_iota(jnp.int32, (LANES, LANES), 0)
    b = lax.broadcasted_iota(jnp.int32, (LANES, LANES), 1)

    def band(first, count, shift):
        return (a >= first) & (a < first + count) & (b == a + shift)

    if kind == 0:
        cross = band(EMB, 64, 0)
        square, unit = QF, 1.0 / 64.0
    else:
        cross = band(XH, 16, 0) | band(XL, 16, XH2 - XL) | band(XH2, 16, XL - XH2)
        square, unit = QX, 1.0
    norms = band(square, 3, ONE - square) | band(ONE, 3, square - ONE)
    return jnp.where(cross, -2.0 * unit, jnp.where(norms, unit, 0.0)).astype(BF16)


def split3(value):
    hi = value.astype(BF16).astype(F32)
    mid = (value - hi).astype(BF16).astype(F32)
    low = (value - hi - mid).astype(BF16).astype(F32)
    return hi, mid, low


def pack_kernel(emb_ref, crd_ref, own_ref, out_ref):
    emb = emb_ref[...].astype(F32)
    crd = crd_ref[...]
    points = emb.shape[1]
    hi = crd.astype(BF16).astype(F32)
    low = (crd - hi).astype(BF16).astype(F32)
    squares = split3(jnp.sum(emb * emb, axis=0, keepdims=True))
    squares += split3(jnp.sum(crd * crd, axis=0, keepdims=True))
    lane = lax.broadcasted_iota(jnp.int32, (16, points), 0)
    tail = jnp.where((lane >= ONE - QF) & (lane < ONE - QF + 3), 1.0, 0.0)
    for k, sq in enumerate(squares):
        tail = jnp.where(lane == k, sq, tail)
    rows = jnp.concatenate([emb, hi, low, hi, tail], axis=0)
    mine = rows.T.astype(BF16)
    own_ref[...] = mine
    for k in range(out_ref.shape[0]):
        out_ref[k] = mine


def pairs_kernel(row_ref, col_ref, w_hbm, out_ref, w_ref, f_scr, x_scr, sems):
    total_rows = row_ref.shape[0]
    total = col_ref.shape[0]
    tm = min(512, total_rows)
    tn = min(256, total)
    per = tm // 64
    steps = total_rows // tm

    def fetch(i):
        at = pl.ds(i * tm, tm)
        return pltpu.make_async_copy(w_hbm.at[at, :], w_ref.at[at, :], sems.at[i])

    for i in range(steps):
        fetch(i).start()
    all_cols = col_ref[...]
    dims = (((1,), (1,)), ((), ()))
    form_f = bilinear_form(0)
    f_scr[...] = lax.dot_general(form_f, all_cols, dims, preferred_element_type=F32).astype(BF16)
    x_scr[...] = lax.dot_general(bilinear_form(1), all_cols, dims, preferred_element_type=F32).astype(BF16)
    lane = lax.broadcasted_iota(jnp.int32, (tm, LANES), 1)

    def block(i, carry):
        mis, scl = carry
        fetch(i).wait()
        at = pl.ds(pl.multiple_of(i * tm, tm), tm)
        rows = row_ref[at, :]
        acc = jnp.zeros((tm, LANES), F32)
        wacc = jnp.zeros((tm, LANES), F32)
        for start in range(0, total, tn):
            cut = slice(start, start + tn)
            f2 = jnp.dot(rows, f_scr[:, cut], preferred_element_type=F32)
            x2 = jnp.dot(rows, x_scr[:, cut], preferred_element_type=F32)
            wb = w_ref[at, cut]
            w = wb.astype(F32)
            f2 = jnp.maximum(f2, TINY)
            x2 = jnp.maximum(x2, TINY)
            dissim = f2 * lax.rsqrt(f2)
            inv = lax.rsqrt(x2)
            diff = dissim - x2 * inv
            cmat = w * (dissim * jnp.minimum(inv, 1.0) - 1.0)
            mis += jnp.sum((w * (diff * diff)).reshape(tm // 8, 8, tn), axis=0)
            cols = col_ref[cut, :]
            acc += jnp.dot(cmat.astype(BF16), cols, preferred_element_type=F32)
            wacc += jnp.dot(wb, cols, preferred_element_type=F32)
        bent = jnp.dot(rows, form_f, preferred_element_type=F32)
        scl += jnp.sum((bent * wacc).reshape(tm // 8, 8, LANES), axis=0)
        sums = jnp.where(lane == ONE + 1, wacc, acc).T
        pull = sums[XH : XH + 16] + sums[XL : XL + 16]
        rate = sums[ONE : ONE + 1]
        wsum = sums[ONE + 1 : ONE + 2]
        for k in range(per):
            cut = slice(64 * k, 64 * k + 64)
            out_ref[i * per + k, 0:8, :] = jnp.concatenate([pull[0:8, cut], pull[8:16, cut]], axis=1)
            out_ref[i * per + k, 8:9, :] = jnp.concatenate([rate[:, cut], wsum[:, cut]], axis=1)
        return mis, scl

    mis, scl = lax.fori_loop(
        0, steps, block, (jnp.zeros((8, tn), F32), jnp.zeros((8, LANES), F32))
    )
    mis = jnp.sum(mis, axis=0, keepdims=True)
    mis = sum(mis[:, k : k + 128] for k in range(0, tn, 128))
    scl = jnp.sum(scl, axis=0, keepdims=True)
    count = out_ref.shape[0]
    out_ref[:, 9:10, :] = jnp.broadcast_to(mis[None], (count, 1, 128))
    out_ref[:, 10:11, :] = jnp.broadcast_to(scl[None], (count, 1, 128))
    out_ref[:, 11:16, :] = jnp.zeros((count, 5, 128), F32)


def finish_kernel(part_ref, crd_ref, new_ref, share_ref):
    sums = jnp.sum(part_ref[...], axis=0)
    rate = sums[8:9, 0:64]
    wsum = sums[8:9, 64:128]
    pull = jnp.concatenate([sums[0:8, 0:64], sums[0:8, 64:128]], axis=0)
    crd = crd_ref[...]
    new_ref[...] = crd + (rate * crd - pull) / wsum
    share_ref[...] = jnp.broadcast_to(sums[8:16][None], share_ref.shape)


def stress_kernel(part_ref, out_ref):
    sums = jnp.sum(part_ref[...], axis=0)
    out_ref[...] = jnp.sum(sums[1:2], axis=1, keepdims=True) / jnp.sum(sums[2:3], axis=1, keepdims=True)


def column_moves(n_row, n_col, n_depth):
    moves = []
    for row in range(n_row):
        for at in range(n_col * n_depth):
            moves.append((row * n_col * n_depth + at, (at % n_row * n_col + row) * n_depth + at // n_row))
    return moves


def shards(embeddings, coords, pair_weight):
    rows, cols = pair_weight.shape
    points = embeddings.shape[1]
    group = rows // points
    n_row, n_col, n_depth = (lax.axis_size(a) for a in ("row", "col", "depth"))

    packed = pl.pallas_call(
        pack_kernel,
        out_shape=(
            jax.ShapeDtypeStruct((points, LANES), BF16),
            jax.ShapeDtypeStruct((group, points, LANES), BF16),
        ),
        name="pack",
    )(embeddings, coords)
    moved = lax.ppermute(packed[0], ("row", "col", "depth"), column_moves(n_row, n_col, n_depth))
    t_rows = lax.all_to_all(packed[1], ("col", "depth"), 0, 0, tiled=True).reshape(rows, LANES)
    moved, t_rows = lax.optimization_barrier((moved, t_rows))
    moved = jnp.broadcast_to(moved[None], (n_row, points, LANES))
    t_cols = lax.all_to_all(moved, "row", 0, 0, tiled=True).reshape(cols, LANES)

    vmem = pl.BlockSpec(memory_space=pltpu.VMEM)
    parts = pl.pallas_call(
        pairs_kernel,
        in_specs=[vmem, vmem, pl.BlockSpec(memory_space=pltpu.HBM)],
        out_specs=vmem,
        out_shape=jax.ShapeDtypeStruct((group, 16, 128), F32),
        scratch_shapes=[
            pltpu.VMEM((rows, cols), BF16),
            pltpu.VMEM((LANES, cols), BF16),
            pltpu.VMEM((LANES, cols), BF16),
            pltpu.SemaphoreType.DMA((max(1, rows // 512),)),
        ],
        compiler_params=pltpu.CompilerParams(vmem_limit_bytes=57 * 1024 * 1024),
        name="pairs",
    )(t_rows, t_cols, pair_weight)
    parts = lax.all_to_all(parts, ("col", "depth"), 0, 0, tiled=True)
    new_coords, shares = pl.pallas_call(
        finish_kernel,
        out_shape=(
            jax.ShapeDtypeStruct(coords.shape, F32),
            jax.ShapeDtypeStruct((n_row, 8, 128), F32),
        ),
        name="finish",
    )(parts, coords)
    shares = lax.all_to_all(shares, "row", 0, 0, tiled=True)
    stress = pl.pallas_call(
        stress_kernel,
        out_shape=jax.ShapeDtypeStruct((1, 1), F32),
        name="stress",
    )(shares)
    return (new_coords, stress[0, 0])


def solution(mesh):
    placed = (
        P(None, ("row", "col", "depth")),
        P(None, ("row", "col", "depth")),
        P("row", ("col", "depth")),
    )
    return jax.shard_map(
        shards,
        mesh=mesh,
        in_specs=placed,
        out_specs=(P(None, ("row", "col", "depth")), P()),
        check_vma=False,
    )
```

```python
import jax
import jax.numpy as jnp
from jax import lax
from jax.experimental import pallas as pl
from jax.experimental.pallas import tpu as pltpu
from jax.sharding import PartitionSpec as P

F32 = jnp.float32
BF16 = jnp.bfloat16

EMB, XH, XL, XH2, QF, QX, ONE, LANES = 0, 64, 80, 96, 112, 115, 118, 128
TINY = 1e-30


def bilinear_form(kind):
    a = lax.broadcasted_iota(jnp.int32, (LANES, LANES), 0)
    b = lax.broadcasted_iota(jnp.int32, (LANES, LANES), 1)

    def band(first, count, shift):
        return (a >= first) & (a < first + count) & (b == a + shift)

    if kind == 0:
        cross = band(EMB, 64, 0)
        square, unit = QF, 1.0 / 64.0
    else:
        cross = band(XH, 16, 0) | band(XL, 16, XH2 - XL) | band(XH2, 16, XL - XH2)
        square, unit = QX, 1.0
    norms = band(square, 3, ONE - square) | band(ONE, 3, square - ONE)
    return jnp.where(cross, -2.0 * unit, jnp.where(norms, unit, 0.0)).astype(BF16)


def split3(value):
    hi = value.astype(BF16).astype(F32)
    mid = (value - hi).astype(BF16).astype(F32)
    low = (value - hi - mid).astype(BF16).astype(F32)
    return hi, mid, low


def pack_kernel(emb_ref, crd_ref, own_ref, out_ref):
    emb = emb_ref[...].astype(F32)
    crd = crd_ref[...]
    points = emb.shape[1]
    hi = crd.astype(BF16).astype(F32)
    low = (crd - hi).astype(BF16).astype(F32)
    squares = split3(jnp.sum(emb * emb, axis=0, keepdims=True))
    squares += split3(jnp.sum(crd * crd, axis=0, keepdims=True))
    lane = lax.broadcasted_iota(jnp.int32, (16, points), 0)
    tail = jnp.where((lane >= ONE - QF) & (lane < ONE - QF + 3), 1.0, 0.0)
    for k, sq in enumerate(squares):
        tail = jnp.where(lane == k, sq, tail)
    rows = jnp.concatenate([emb, hi, low, hi, tail], axis=0)
    mine = rows.T.astype(BF16)
    own_ref[...] = mine
    for k in range(out_ref.shape[0]):
        out_ref[k] = mine


def pairs_kernel(core_ref, own_ref, oth_ref, col_ref, w_hbm, out_ref, w_ref, f_scr, x_scr, sems):
    total_rows, total = w_ref.shape
    tm = min(1024, total_rows)
    tn = min(256, total)
    steps = total_rows // tm
    first = core_ref[0] == 0

    def fetch(i):
        at = pl.ds(i * tm, tm)
        return pltpu.make_async_copy(w_hbm.at[at, :], w_ref.at[at, :], sems.at[i])

    for i in range(steps):
        fetch(i).start()
    all_cols = col_ref[...]
    dims = (((1,), (1,)), ((), ()))
    form_f = bilinear_form(0)
    f_scr[...] = lax.dot_general(form_f, all_cols, dims, preferred_element_type=F32).astype(BF16)
    x_scr[...] = lax.dot_general(bilinear_form(1), all_cols, dims, preferred_element_type=F32).astype(BF16)
    lane = lax.broadcasted_iota(jnp.int32, (tm, LANES), 1)

    def block(i, carry):
        mis, scl = carry
        fetch(i).wait()
        at = pl.ds(pl.multiple_of(i * tm, tm), tm)
        pieces = []
        for k in range(tm // 256):
            cut = pl.ds(pl.multiple_of(i * (tm // 2) + k * 128, 128), 128)
            own, oth = own_ref[cut, :], oth_ref[cut, :]
            pieces += [jnp.where(first, own, oth), jnp.where(first, oth, own)]
        rows = jnp.concatenate(pieces, axis=0)
        acc = jnp.zeros((2 * tm, LANES), F32)
        for start in range(0, total, tn):
            cut = slice(start, start + tn)
            f2 = jnp.dot(rows, f_scr[:, cut], preferred_element_type=F32)
            x2 = jnp.dot(rows, x_scr[:, cut], preferred_element_type=F32)
            wb = w_ref[at, cut]
            w = wb.astype(F32)
            f2 = jnp.maximum(f2, TINY)
            x2 = jnp.maximum(x2, TINY)
            dissim = f2 * lax.rsqrt(f2)
            inv = lax.rsqrt(x2)
            diff = dissim - x2 * inv
            cmat = w * (dissim * jnp.minimum(inv, 1.0) - 1.0)
            mis += jnp.sum((w * (diff * diff)).reshape(tm // 8, 8, tn), axis=0)
            both = jnp.concatenate([cmat.astype(BF16), wb], axis=0)
            acc += jnp.dot(both, col_ref[cut, :], preferred_element_type=F32)
        bent = jnp.dot(rows, form_f, preferred_element_type=F32)
        scl += jnp.sum((bent * acc[tm:]).reshape(tm // 8, 8, LANES), axis=0)
        sums = jnp.where(lane == ONE + 1, acc[tm:], acc[:tm]).T
        pull = sums[XH : XH + 16] + sums[XL : XL + 16]
        rate = sums[ONE : ONE + 1]
        wsum = sums[ONE + 1 : ONE + 2]
        for k in range(tm // 64):
            cut = slice(64 * k, 64 * k + 64)
            to = i * (tm // 64) + k
            for j in range(8):
                line = jnp.concatenate([pull[j : j + 1, cut], pull[j + 8 : j + 9, cut]], axis=1)
                out_ref[to, :, 128 * j : 128 * j + 128] = line
            out_ref[to, :, 1024:1152] = jnp.concatenate([rate[:, cut], wsum[:, cut]], axis=1)
        return mis, scl

    mis, scl = lax.fori_loop(
        0, steps, block, (jnp.zeros((8, tn), F32), jnp.zeros((8, LANES), F32))
    )
    mis = jnp.sum(jnp.sum(mis, axis=0, keepdims=True), axis=1, keepdims=True)
    scl = jnp.sum(jnp.sum(scl, axis=0, keepdims=True), axis=1, keepdims=True)
    at = lax.broadcasted_iota(jnp.int32, (1, 128), 1)
    line = jnp.where(at == 0, mis, jnp.where(at == 1, scl, 0.0))
    out_ref[:, :, 1152:1280] = jnp.broadcast_to(line[None], (out_ref.shape[0], 1, 128))


def finish_kernel(part_ref, crd_ref, new_ref, share_ref):
    sums = jnp.sum(part_ref[...], axis=0)
    lines = [sums[:, 128 * k : 128 * k + 128] for k in range(10)]
    share_ref[...] = jnp.broadcast_to(lines[9][None], share_ref.shape)
    half = jnp.concatenate(lines[:8], axis=0)
    pull = jnp.concatenate([half[:, 0:64], half[:, 64:128]], axis=0)
    rate = lines[8][:, 0:64]
    wsum = lines[8][:, 64:128]
    crd = crd_ref[...]
    new_ref[...] = crd + (rate * crd - pull) / wsum


def stress_kernel(part_ref, out_ref):
    sums = jnp.sum(part_ref[...], axis=0)
    out_ref[...] = sums[:, 0:1] / sums[:, 1:2]


def column_moves(n_row, n_col, n_depth):
    moves = []
    for row in range(n_row):
        for at in range(n_col * n_depth):
            moves.append((row * n_col * n_depth + at, (at % n_row * n_col + row) * n_depth + at // n_row))
    return moves


def shards(embeddings, coords, pair_weight):
    rows, cols = pair_weight.shape
    points = embeddings.shape[1]
    group = rows // points
    n_row, n_z, n_core, n_depth = (lax.axis_size(a) for a in ("row", "z", "core", "depth"))
    likes = n_z * n_depth

    packed = pl.pallas_call(
        pack_kernel,
        out_shape=(
            jax.ShapeDtypeStruct((points, LANES), BF16),
            jax.ShapeDtypeStruct((likes, points, LANES), BF16),
        ),
        name="pack",
    )(embeddings, coords)
    moves = column_moves(n_row, n_z * n_core, n_depth)
    moved = lax.ppermute(packed[0], ("row", "z", "core", "depth"), moves)
    own = lax.all_to_all(packed[1], ("z", "depth"), 0, 0, tiled=True).reshape(rows // n_core, LANES)
    moved, own = lax.optimization_barrier((moved, own))
    oth = lax.ppermute(own, "core", [(0, 1), (1, 0)])
    moved = jnp.broadcast_to(moved[None], (n_row, points, LANES))
    t_cols = lax.all_to_all(moved, "row", 0, 0, tiled=True).reshape(cols, LANES)

    vmem = pl.BlockSpec(memory_space=pltpu.VMEM)
    parts = pl.pallas_call(
        pairs_kernel,
        in_specs=[
            pl.BlockSpec(memory_space=pltpu.SMEM),
            vmem,
            vmem,
            vmem,
            pl.BlockSpec(memory_space=pltpu.HBM),
        ],
        out_specs=vmem,
        out_shape=jax.ShapeDtypeStruct((group, 1, 1280), F32),
        scratch_shapes=[
            pltpu.VMEM((rows, cols), BF16),
            pltpu.VMEM((LANES, cols), BF16),
            pltpu.VMEM((LANES, cols), BF16),
            pltpu.SemaphoreType.DMA((max(1, rows // 1024),)),
        ],
        compiler_params=pltpu.CompilerParams(vmem_limit_bytes=52 * 1024 * 1024),
        name="pairs",
    )(lax.axis_index("core").reshape(1).astype(jnp.int32), own, oth, t_cols, pair_weight)
    parts = lax.all_to_all(parts, ("z", "core", "depth"), 0, 0, tiled=True)
    new_coords, shares = pl.pallas_call(
        finish_kernel,
        out_shape=(
            jax.ShapeDtypeStruct(coords.shape, F32),
            jax.ShapeDtypeStruct((n_row, 1, 128), F32),
        ),
        name="finish",
    )(parts, coords)
    shares = lax.all_to_all(shares, "row", 0, 0, tiled=True)
    stress = pl.pallas_call(
        stress_kernel,
        out_shape=jax.ShapeDtypeStruct((1, 1), F32),
        name="stress",
    )(shares)
    return (new_coords, stress[0, 0])


def solution(mesh):
    n_row, n_col, n_depth = (mesh.shape[a] for a in ("row", "col", "depth"))
    fine = jax.sharding.Mesh(
        mesh.devices.reshape(n_row, n_col // 2, 2, n_depth), ("row", "z", "core", "depth")
    )
    points = P(None, ("row", "z", "core", "depth"))
    return jax.shard_map(
        shards,
        mesh=fine,
        in_specs=(points, points, P("row", ("z", "core", "depth"))),
        out_specs=(points, P()),
        check_vma=False,
    )
```

```python
import jax
import jax.numpy as jnp
from jax import lax
from jax.experimental import pallas as pl
from jax.experimental.pallas import tpu as pltpu
from jax.sharding import PartitionSpec as P

F32 = jnp.float32
BF16 = jnp.bfloat16

EMB, XH, XL, XH2, QF, QX, ONE, LANES = 0, 64, 80, 96, 112, 115, 118, 128
TINY = 1e-30


def bilinear_form(kind):
    a = lax.broadcasted_iota(jnp.int32, (LANES, LANES), 0)
    b = lax.broadcasted_iota(jnp.int32, (LANES, LANES), 1)

    def band(first, count, shift):
        return (a >= first) & (a < first + count) & (b == a + shift)

    if kind == 0:
        cross = band(EMB, 64, 0)
        square, unit = QF, 1.0 / 64.0
    else:
        cross = band(XH, 16, 0) | band(XL, 16, XH2 - XL) | band(XH2, 16, XL - XH2)
        square, unit = QX, 1.0
    norms = band(square, 3, ONE - square) | band(ONE, 3, square - ONE)
    return jnp.where(cross, -2.0 * unit, jnp.where(norms, unit, 0.0)).astype(BF16)


def split3(value):
    hi = value.astype(BF16).astype(F32)
    mid = (value - hi).astype(BF16).astype(F32)
    low = (value - hi - mid).astype(BF16).astype(F32)
    return hi, mid, low


def pack_kernel(emb_ref, crd_ref, own_ref, out_ref):
    emb = emb_ref[...].astype(F32)
    crd = crd_ref[...]
    points = emb.shape[1]
    hi = crd.astype(BF16).astype(F32)
    low = (crd - hi).astype(BF16).astype(F32)
    squares = split3(jnp.sum(emb * emb, axis=0, keepdims=True))
    squares += split3(jnp.sum(crd * crd, axis=0, keepdims=True))
    lane = lax.broadcasted_iota(jnp.int32, (16, points), 0)
    tail = jnp.where((lane >= ONE - QF) & (lane < ONE - QF + 3), 1.0, 0.0)
    for k, sq in enumerate(squares):
        tail = jnp.where(lane == k, sq, tail)
    rows = jnp.concatenate([emb, hi, low, hi, tail], axis=0)
    mine = rows.T.astype(BF16)
    own_ref[...] = mine
    for k in range(out_ref.shape[0]):
        out_ref[k] = mine


def pick_sums():
    a = lax.broadcasted_iota(jnp.int32, (48, LANES), 0)
    b = lax.broadcasted_iota(jnp.int32, (48, LANES), 1)
    keep = ((a < 32) & (b == a + XH)) | ((a >= 32) & (b == ONE))
    return jnp.where(keep, 1.0, 0.0).astype(BF16)


def pairs_kernel(core_ref, own_ref, oth_ref, col_ref, w_hbm, out_ref, w_ref, f_scr, x_scr, sems):
    total_rows, total = w_ref.shape
    tm = min(1024, total_rows)
    tn = min(256, total)
    steps = total_rows // tm
    first = core_ref[0] == 0

    def fetch(i):
        at = pl.ds(i * tm, tm)
        return pltpu.make_async_copy(w_hbm.at[at, :], w_ref.at[at, :], sems.at[i])

    for i in range(steps):
        fetch(i).start()
    all_cols = col_ref[...]
    last = (((1,), (1,)), ((), ()))
    f_scr[...] = lax.dot_general(bilinear_form(0), all_cols, last, preferred_element_type=F32).astype(BF16)
    x_scr[...] = lax.dot_general(bilinear_form(1), all_cols, last, preferred_element_type=F32).astype(BF16)
    flat = lax.dot_general(pick_sums(), all_cols, last, preferred_element_type=F32).astype(BF16)

    def block(i, carry):
        mis, scl = carry
        fetch(i).wait()
        at = pl.ds(pl.multiple_of(i * tm, tm), tm)
        pieces = []
        for k in range(tm // 256):
            cut = pl.ds(pl.multiple_of(i * (tm // 2) + k * 128, 128), 128)
            own, oth = own_ref[cut, :], oth_ref[cut, :]
            pieces += [jnp.where(first, own, oth), jnp.where(first, oth, own)]
        rows = jnp.concatenate(pieces, axis=0)
        acc = jnp.zeros((48, tm), F32)
        wacc = jnp.zeros((16, tm), F32)
        for start in range(0, total, tn):
            cut = slice(start, start + tn)
            f2 = jnp.dot(rows, f_scr[:, cut], preferred_element_type=F32)
            x2 = jnp.dot(rows, x_scr[:, cut], preferred_element_type=F32)
            wb = w_ref[at, cut]
            w = wb.astype(F32)
            f2 = jnp.maximum(f2, TINY)
            x2 = jnp.maximum(x2, TINY)
            dissim = f2 * lax.rsqrt(f2)
            inv = lax.rsqrt(x2)
            diff = dissim - x2 * inv
            cmat = w * (dissim * jnp.minimum(inv, 1.0) - 1.0)
            mis += jnp.sum((w * (diff * diff)).reshape(tm // 8, 8, tn), axis=0)
            scl += jnp.sum((w * f2).reshape(tm // 8, 8, tn), axis=0)
            acc += lax.dot_general(flat[:, cut], cmat.astype(BF16), last, preferred_element_type=F32)
            wacc += lax.dot_general(flat[32:, cut], wb, last, preferred_element_type=F32)
        pull = acc[0:16] + acc[16:32]
        rate = acc[32:33]
        wsum = wacc[0:1]
        for k in range(tm // 64):
            cut = slice(64 * k, 64 * k + 64)
            to = i * (tm // 64) + k
            for j in range(8):
                line = jnp.concatenate([pull[j : j + 1, cut], pull[j + 8 : j + 9, cut]], axis=1)
                out_ref[to, :, 128 * j : 128 * j + 128] = line
            out_ref[to, :, 1024:1152] = jnp.concatenate([rate[:, cut], wsum[:, cut]], axis=1)
        return mis, scl

    zero = jnp.zeros((8, tn), F32)
    mis, scl = lax.fori_loop(0, steps, block, (zero, zero))
    mis = jnp.sum(jnp.sum(mis, axis=0, keepdims=True), axis=1, keepdims=True)
    scl = jnp.sum(jnp.sum(scl, axis=0, keepdims=True), axis=1, keepdims=True)
    at = lax.broadcasted_iota(jnp.int32, (1, 128), 1)
    line = jnp.where(at == 0, mis, jnp.where(at == 1, scl, 0.0))
    out_ref[:, :, 1152:1280] = jnp.broadcast_to(line[None], (out_ref.shape[0], 1, 128))


def finish_kernel(part_ref, crd_ref, new_ref):
    sums = jnp.sum(part_ref[...], axis=0)
    lines = [sums[:, 128 * k : 128 * k + 128] for k in range(9)]
    half = jnp.concatenate(lines[:8], axis=0)
    pull = jnp.concatenate([half[:, 0:64], half[:, 64:128]], axis=0)
    rate = lines[8][:, 0:64]
    wsum = lines[8][:, 64:128]
    crd = crd_ref[...]
    new_ref[...] = crd + (rate * crd - pull) / wsum


def stress_kernel(part_ref, out_ref):
    sums = jnp.sum(part_ref[...], axis=0)
    out_ref[...] = sums[:, 0:1] / sums[:, 1:2]


def column_moves(n_row, n_col, n_depth):
    moves = []
    for row in range(n_row):
        for at in range(n_col * n_depth):
            moves.append((row * n_col * n_depth + at, (at % n_row * n_col + row) * n_depth + at // n_row))
    return moves


def shards(embeddings, coords, pair_weight):
    rows, cols = pair_weight.shape
    points = embeddings.shape[1]
    group = rows // points
    n_row, n_z, n_core, n_depth = (lax.axis_size(a) for a in ("row", "z", "core", "depth"))
    likes = n_z * n_depth

    packed = pl.pallas_call(
        pack_kernel,
        out_shape=(
            jax.ShapeDtypeStruct((points, LANES), BF16),
            jax.ShapeDtypeStruct((likes, points, LANES), BF16),
        ),
        name="pack",
    )(embeddings, coords)
    moves = column_moves(n_row, n_z * n_core, n_depth)
    moved = lax.ppermute(packed[0], ("row", "z", "core", "depth"), moves)
    own = lax.all_to_all(packed[1], ("z", "depth"), 0, 0, tiled=True).reshape(rows // n_core, LANES)
    moved, own = lax.optimization_barrier((moved, own))
    oth = lax.ppermute(own, "core", [(0, 1), (1, 0)])
    moved = jnp.broadcast_to(moved[None], (n_row, points, LANES))
    t_cols = lax.all_to_all(moved, "row", 0, 0, tiled=True).reshape(cols, LANES)

    vmem = pl.BlockSpec(memory_space=pltpu.VMEM)
    parts = pl.pallas_call(
        pairs_kernel,
        in_specs=[
            pl.BlockSpec(memory_space=pltpu.SMEM),
            vmem,
            vmem,
            vmem,
            pl.BlockSpec(memory_space=pltpu.HBM),
        ],
        out_specs=vmem,
        out_shape=jax.ShapeDtypeStruct((group, 1, 1280), F32),
        scratch_shapes=[
            pltpu.VMEM((rows, cols), BF16),
            pltpu.VMEM((LANES, cols), BF16),
            pltpu.VMEM((LANES, cols), BF16),
            pltpu.SemaphoreType.DMA((max(1, rows // 1024),)),
        ],
        compiler_params=pltpu.CompilerParams(vmem_limit_bytes=52 * 1024 * 1024),
        name="pairs",
    )(lax.axis_index("core").reshape(1).astype(jnp.int32), own, oth, t_cols, pair_weight)
    parts = lax.all_to_all(parts, ("z", "core", "depth"), 0, 0, tiled=True)
    shares = jnp.sum(parts[:, :, 1152:], axis=0, keepdims=True)
    shares = lax.all_to_all(jnp.broadcast_to(shares, (n_row, 1, 128)), "row", 0, 0, tiled=True)
    new_coords = pl.pallas_call(
        finish_kernel,
        out_shape=jax.ShapeDtypeStruct(coords.shape, F32),
        cost_estimate=pl.CostEstimate(flops=100000, bytes_accessed=200000, transcendentals=0),
        name="finish",
    )(parts, coords)
    stress = pl.pallas_call(
        stress_kernel,
        out_shape=jax.ShapeDtypeStruct((1, 1), F32),
        name="stress",
    )(shares)
    return (new_coords, stress[0, 0])


def solution(mesh):
    n_row, n_col, n_depth = (mesh.shape[a] for a in ("row", "col", "depth"))
    fine = jax.sharding.Mesh(
        mesh.devices.reshape(n_row, n_col // 2, 2, n_depth), ("row", "z", "core", "depth")
    )
    points = P(None, ("row", "z", "core", "depth"))
    return jax.shard_map(
        shards,
        mesh=fine,
        in_specs=(points, points, P("row", ("z", "core", "depth"))),
        out_specs=(points, P()),
        check_vma=False,
    )
```

```python
import jax
import jax.numpy as jnp
from jax import lax
from jax.experimental import pallas as pl
from jax.experimental.pallas import tpu as pltpu
from jax.sharding import PartitionSpec as P

F32 = jnp.float32
BF16 = jnp.bfloat16

EMB, XH, XL, XH2, QF, QX, ONE, LANES = 0, 64, 80, 96, 112, 115, 118, 128
TINY = 1e-30


def bilinear_form(kind):
    a = lax.broadcasted_iota(jnp.int32, (LANES, LANES), 0)
    b = lax.broadcasted_iota(jnp.int32, (LANES, LANES), 1)

    def band(first, count, shift):
        return (a >= first) & (a < first + count) & (b == a + shift)

    if kind == 0:
        cross = band(EMB, 64, 0)
        square, unit = QF, 1.0 / 64.0
    else:
        cross = band(XH, 16, 0) | band(XL, 16, XH2 - XL) | band(XH2, 16, XL - XH2)
        square, unit = QX, 1.0
    norms = band(square, 3, ONE - square) | band(ONE, 3, square - ONE)
    return jnp.where(cross, -2.0 * unit, jnp.where(norms, unit, 0.0)).astype(BF16)


def split3(value):
    hi = value.astype(BF16).astype(F32)
    mid = (value - hi).astype(BF16).astype(F32)
    low = (value - hi - mid).astype(BF16).astype(F32)
    return hi, mid, low


def pack_kernel(emb_ref, crd_ref, own_ref, out_ref):
    emb = emb_ref[...].astype(F32)
    crd = crd_ref[...]
    points = emb.shape[1]
    hi = crd.astype(BF16).astype(F32)
    low = (crd - hi).astype(BF16).astype(F32)
    squares = split3(jnp.sum(emb * emb, axis=0, keepdims=True))
    squares += split3(jnp.sum(crd * crd, axis=0, keepdims=True))
    lane = lax.broadcasted_iota(jnp.int32, (16, points), 0)
    tail = jnp.where((lane >= ONE - QF) & (lane < ONE - QF + 3), 1.0, 0.0)
    for k, sq in enumerate(squares):
        tail = jnp.where(lane == k, sq, tail)
    rows = jnp.concatenate([emb, hi, low, hi, tail], axis=0)
    mine = rows.T.astype(BF16)
    own_ref[...] = mine
    for k in range(out_ref.shape[0]):
        out_ref[k] = mine


def pick_sums():
    a = lax.broadcasted_iota(jnp.int32, (48, LANES), 0)
    b = lax.broadcasted_iota(jnp.int32, (48, LANES), 1)
    keep = ((a < 32) & (b == a + XH)) | ((a >= 32) & (b == ONE))
    return jnp.where(keep, 1.0, 0.0).astype(BF16)


def pairs_kernel(own_ref, oth_ref, col_ref, w_hbm, out_ref, w_ref, f_scr, x_scr, flat_scr, c_scr, f_tiles, x_tiles, sems):
    total_rows, total = w_ref.shape
    tm = c_scr.shape[0]
    tn = min(256, total)
    steps = total_rows // tm
    first = lax.axis_index("core") == 0

    def fetch(i):
        at = pl.ds(i * tm, tm)
        return pltpu.make_async_copy(w_hbm.at[at, :], w_ref.at[at, :], sems.at[i])

    for i in range(steps):
        fetch(i).start()
    all_cols = col_ref[...]
    last = (((1,), (1,)), ((), ()))
    f_scr[...] = lax.dot_general(bilinear_form(0), all_cols, last, preferred_element_type=F32).astype(BF16)
    x_scr[...] = lax.dot_general(bilinear_form(1), all_cols, last, preferred_element_type=F32).astype(BF16)
    flat_scr[...] = lax.dot_general(pick_sums(), all_cols, last, preferred_element_type=F32).astype(BF16)

    def squares(i, slot):
        pieces = []
        for k in range(tm // 256):
            cut = pl.ds(pl.multiple_of(i * (tm // 2) + k * 128, 128), 128)
            own, oth = own_ref[cut, :], oth_ref[cut, :]
            pieces += [jnp.where(first, own, oth), jnp.where(first, oth, own)]
        rows = jnp.concatenate(pieces, axis=0)
        f_tiles[slot] = jnp.dot(rows, f_scr[...], preferred_element_type=F32)
        x_tiles[slot] = jnp.dot(rows, x_scr[...], preferred_element_type=F32)

    def block(i, slot, mis, scl):
        fetch(i).wait()
        squares(jnp.minimum(i + 1, steps - 1), 1 - slot)
        base = i * tm
        acc = jnp.zeros((48, tm), F32)
        wacc = jnp.zeros((16, tm), F32)
        for start in range(0, total, tn):
            cut = slice(start, start + tn)
            for r in range(0, tm, 16):
                f2 = jnp.maximum(f_tiles[slot, r : r + 16, cut], TINY)
                x2 = jnp.maximum(x_tiles[slot, r : r + 16, cut], TINY)
                w = w_ref[pl.ds(pl.multiple_of(base + r, 16), 16), cut].astype(F32)
                dissim = f2 * lax.rsqrt(f2)
                inv = lax.rsqrt(x2)
                diff = dissim - x2 * inv
                cmat = w * (dissim * jnp.minimum(inv, 1.0) - 1.0)
                c_scr[r : r + 16, cut] = cmat.astype(BF16)
                miss = w * (diff * diff)
                size = w * f2
                mis += miss[0:8] + miss[8:16]
                scl += size[0:8] + size[8:16]
            wb = w_ref[pl.ds(pl.multiple_of(base, tm), tm), cut]
            acc += lax.dot_general(flat_scr[:, cut], c_scr[:, cut], last, preferred_element_type=F32)
            wacc += lax.dot_general(flat_scr[32:, cut], wb, last, preferred_element_type=F32)
        pull = acc[0:16] + acc[16:32]
        rate = acc[32:33]
        wsum = wacc[0:1]
        for k in range(tm // 64):
            cut = slice(64 * k, 64 * k + 64)
            to = i * (tm // 64) + k
            for j in range(8):
                line = jnp.concatenate([pull[j : j + 1, cut], pull[j + 8 : j + 9, cut]], axis=1)
                out_ref[to, :, 128 * j : 128 * j + 128] = line
            out_ref[to, :, 1024:1152] = jnp.concatenate([rate[:, cut], wsum[:, cut]], axis=1)
        return mis, scl

    def two(k, carry):
        carry = block(2 * k, 0, *carry)
        return block(2 * k + 1, 1, *carry)

    squares(0, 0)
    zero = jnp.zeros((8, tn), F32)
    mis, scl = lax.fori_loop(0, steps // 2, two, (zero, zero))
    if steps % 2:
        mis, scl = block(steps - 1, 0, mis, scl)
    mis = jnp.sum(jnp.sum(mis, axis=0, keepdims=True), axis=1, keepdims=True)
    scl = jnp.sum(jnp.sum(scl, axis=0, keepdims=True), axis=1, keepdims=True)
    at = lax.broadcasted_iota(jnp.int32, (1, 128), 1)
    line = jnp.where(at == 0, mis, jnp.where(at == 1, scl, 0.0))
    out_ref[:, :, 1152:1280] = jnp.broadcast_to(line[None], (out_ref.shape[0], 1, 128))


def finish_kernel(part_ref, crd_ref, new_ref):
    sums = jnp.sum(part_ref[...], axis=0)
    lines = [sums[:, 128 * k : 128 * k + 128] for k in range(9)]
    half = jnp.concatenate(lines[:8], axis=0)
    pull = jnp.concatenate([half[:, 0:64], half[:, 64:128]], axis=0)
    rate = lines[8][:, 0:64]
    wsum = lines[8][:, 64:128]
    crd = crd_ref[...]
    new_ref[...] = crd + (rate * crd - pull) / wsum


def column_moves(n_row, n_col, n_depth):
    moves = []
    for row in range(n_row):
        for at in range(n_col * n_depth):
            moves.append((row * n_col * n_depth + at, (at % n_row * n_col + row) * n_depth + at // n_row))
    return moves


def shards(embeddings, coords, pair_weight):
    rows, cols = pair_weight.shape
    points = embeddings.shape[1]
    group = rows // points
    n_row, n_z, n_core, n_depth = (lax.axis_size(a) for a in ("row", "z", "core", "depth"))
    likes = n_z * n_depth

    packed = pl.pallas_call(
        pack_kernel,
        out_shape=(
            jax.ShapeDtypeStruct((points, LANES), BF16),
            jax.ShapeDtypeStruct((likes, points, LANES), BF16),
        ),
        name="pack",
    )(embeddings, coords)
    moves = column_moves(n_row, n_z * n_core, n_depth)
    moved = lax.ppermute(packed[0], ("row", "z", "core", "depth"), moves)
    own = lax.all_to_all(packed[1], ("z", "depth"), 0, 0, tiled=True).reshape(rows // n_core, LANES)
    moved, own = lax.optimization_barrier((moved, own))
    oth = lax.ppermute(own, "core", [(0, 1), (1, 0)])
    moved = jnp.broadcast_to(moved[None], (n_row, points, LANES))
    t_cols = lax.all_to_all(moved, "row", 0, 0, tiled=True).reshape(cols, LANES)

    vmem = pl.BlockSpec(memory_space=pltpu.VMEM)
    tm = 256
    parts = pl.pallas_call(
        pairs_kernel,
        in_specs=[
            vmem,
            vmem,
            vmem,
            pl.BlockSpec(memory_space=pltpu.HBM),
        ],
        out_specs=vmem,
        out_shape=jax.ShapeDtypeStruct((group, 1, 1280), F32),
        scratch_shapes=[
            pltpu.VMEM((rows, cols), BF16),
            pltpu.VMEM((LANES, cols), BF16),
            pltpu.VMEM((LANES, cols), BF16),
            pltpu.VMEM((48, cols), BF16),
            pltpu.VMEM((tm, cols), BF16),
            pltpu.VMEM((2, tm, cols), F32),
            pltpu.VMEM((2, tm, cols), F32),
            pltpu.SemaphoreType.DMA((rows // tm,)),
        ],
        compiler_params=pltpu.CompilerParams(vmem_limit_bytes=52 * 1024 * 1024),
        name="pairs",
    )(own, oth, t_cols, pair_weight)
    parts = lax.all_to_all(parts, ("z", "core", "depth"), 0, 0, tiled=True)
    shares = jnp.sum(parts[:, :, 1152:], axis=0, keepdims=True)
    shares = lax.all_to_all(jnp.broadcast_to(shares, (n_row, 1, 128)), "row", 0, 0, tiled=True)
    new_coords = pl.pallas_call(
        finish_kernel,
        out_shape=jax.ShapeDtypeStruct(coords.shape, F32),
        cost_estimate=pl.CostEstimate(flops=100000, bytes_accessed=200000, transcendentals=0),
        name="finish",
    )(parts, coords)
    totals = jnp.sum(shares, axis=(0, 1))
    return (new_coords, totals[0] / totals[1])


def solution(mesh):
    n_row, n_col, n_depth = (mesh.shape[a] for a in ("row", "col", "depth"))
    fine = jax.sharding.Mesh(
        mesh.devices.reshape(n_row, n_col // 2, 2, n_depth), ("row", "z", "core", "depth")
    )
    points = P(None, ("row", "z", "core", "depth"))
    return jax.shard_map(
        shards,
        mesh=fine,
        in_specs=(points, points, P("row", ("z", "core", "depth"))),
        out_specs=(points, P()),
        check_vma=False,
    )
```

```python
import jax
import jax.numpy as jnp
from jax import lax
from jax.experimental import pallas as pl
from jax.experimental.pallas import tpu as pltpu
from jax.sharding import PartitionSpec as P

F32 = jnp.float32
BF16 = jnp.bfloat16

EMB, XH, XL, XH2, QF, QX, ONE, LANES = 0, 64, 80, 96, 112, 115, 118, 128
TINY = 1e-30


def bilinear_form(kind):
    a = lax.broadcasted_iota(jnp.int32, (LANES, LANES), 0)
    b = lax.broadcasted_iota(jnp.int32, (LANES, LANES), 1)

    def band(first, count, shift):
        return (a >= first) & (a < first + count) & (b == a + shift)

    if kind == 0:
        cross = band(EMB, 64, 0)
        square, unit = QF, 1.0 / 64.0
    else:
        cross = band(XH, 16, 0) | band(XL, 16, XH2 - XL) | band(XH2, 16, XL - XH2)
        square, unit = QX, 1.0
    norms = band(square, 3, ONE - square) | band(ONE, 3, square - ONE)
    return jnp.where(cross, -2.0 * unit, jnp.where(norms, unit, 0.0)).astype(BF16)


def split3(value):
    hi = value.astype(BF16).astype(F32)
    mid = (value - hi).astype(BF16).astype(F32)
    low = (value - hi - mid).astype(BF16).astype(F32)
    return hi, mid, low


def pack_kernel(emb_ref, crd_ref, own_ref):
    emb = emb_ref[...].astype(F32)
    crd = crd_ref[...]
    points = emb.shape[1]
    hi = crd.astype(BF16).astype(F32)
    low = (crd - hi).astype(BF16).astype(F32)
    squares = split3(jnp.sum(emb * emb, axis=0, keepdims=True))
    squares += split3(jnp.sum(crd * crd, axis=0, keepdims=True))
    lane = lax.broadcasted_iota(jnp.int32, (16, points), 0)
    tail = jnp.where((lane >= ONE - QF) & (lane < ONE - QF + 3), 1.0, 0.0)
    for k, sq in enumerate(squares):
        tail = jnp.where(lane == k, sq, tail)
    rows = jnp.concatenate([emb, hi, low, hi, tail], axis=0)
    own_ref[...] = rows.T.astype(BF16)


def pick_sums():
    a = lax.broadcasted_iota(jnp.int32, (48, LANES), 0)
    b = lax.broadcasted_iota(jnp.int32, (48, LANES), 1)
    keep = ((a < 32) & (b == a + XH)) | ((a >= 32) & (b == ONE))
    return jnp.where(keep, 1.0, 0.0).astype(BF16)


def pairs_kernel(own_ref, oth_ref, col_ref, w_hbm, out_ref, w_ref, f_scr, x_scr, flat_scr, c_scr, f_tiles, x_tiles, sems):
    total_rows, total = w_ref.shape
    tm = c_scr.shape[0]
    tn = min(256, total)
    steps = total_rows // tm
    first = lax.axis_index("core") == 0

    def fetch(i):
        at = pl.ds(i * tm, tm)
        return pltpu.make_async_copy(w_hbm.at[at, :], w_ref.at[at, :], sems.at[i])

    for i in range(steps):
        fetch(i).start()
    all_cols = col_ref[...]
    last = (((1,), (1,)), ((), ()))
    f_scr[...] = lax.dot_general(bilinear_form(0), all_cols, last, preferred_element_type=F32).astype(BF16)
    x_scr[...] = lax.dot_general(bilinear_form(1), all_cols, last, preferred_element_type=F32).astype(BF16)
    flat_scr[...] = lax.dot_general(pick_sums(), all_cols, last, preferred_element_type=F32).astype(BF16)

    def squares(i, slot):
        pieces = []
        for k in range(tm // 256):
            cut = pl.ds(pl.multiple_of(i * (tm // 2) + k * 128, 128), 128)
            own, oth = own_ref[cut, :], oth_ref[cut, :]
            pieces += [jnp.where(first, own, oth), jnp.where(first, oth, own)]
        rows = jnp.concatenate(pieces, axis=0)
        f_tiles[slot] = jnp.dot(rows, f_scr[...], preferred_element_type=F32)
        x_tiles[slot] = jnp.dot(rows, x_scr[...], preferred_element_type=F32)

    def block(i, slot, mis, scl):
        fetch(i).wait()
        squares(jnp.minimum(i + 1, steps - 1), 1 - slot)
        base = i * tm
        acc = jnp.zeros((48, tm), F32)
        wacc = jnp.zeros((16, tm), F32)
        for start in range(0, total, tn):
            cut = slice(start, start + tn)
            for r in range(0, tm, 16):
                f2 = jnp.maximum(f_tiles[slot, r : r + 16, cut], TINY)
                x2 = jnp.maximum(x_tiles[slot, r : r + 16, cut], TINY)
                w = w_ref[pl.ds(pl.multiple_of(base + r, 16), 16), cut].astype(F32)
                log_f = jnp.log(f2) * 0.5
                log_x = jnp.log(x2) * 0.5
                diff = jnp.exp(log_f) - jnp.exp(log_x)
                cmat = w * (jnp.exp(log_f - jnp.maximum(log_x, 0.0)) - 1.0)
                c_scr[r : r + 16, cut] = cmat.astype(BF16)
                miss = w * (diff * diff)
                size = w * f2
                mis += miss[0:8] + miss[8:16]
                scl += size[0:8] + size[8:16]
            wb = w_ref[pl.ds(pl.multiple_of(base, tm), tm), cut]
            acc += lax.dot_general(flat_scr[:, cut], c_scr[:, cut], last, preferred_element_type=F32)
            wacc += lax.dot_general(flat_scr[32:, cut], wb, last, preferred_element_type=F32)
        pull = acc[0:16] + acc[16:32]
        rate = acc[32:33]
        wsum = wacc[0:1]
        for k in range(tm // 64):
            cut = slice(64 * k, 64 * k + 64)
            to = i * (tm // 64) + k
            for j in range(8):
                line = jnp.concatenate([pull[j : j + 1, cut], pull[j + 8 : j + 9, cut]], axis=1)
                out_ref[to, :, 128 * j : 128 * j + 128] = line
            out_ref[to, :, 1024:1152] = jnp.concatenate([rate[:, cut], wsum[:, cut]], axis=1)
        return mis, scl

    def two(k, carry):
        carry = block(2 * k, 0, *carry)
        return block(2 * k + 1, 1, *carry)

    squares(0, 0)
    zero = jnp.zeros((8, tn), F32)
    mis, scl = lax.fori_loop(0, steps // 2, two, (zero, zero))
    if steps % 2:
        mis, scl = block(steps - 1, 0, mis, scl)
    mis = jnp.sum(jnp.sum(mis, axis=0, keepdims=True), axis=1, keepdims=True)
    scl = jnp.sum(jnp.sum(scl, axis=0, keepdims=True), axis=1, keepdims=True)
    at = lax.broadcasted_iota(jnp.int32, (1, 128), 1)
    line = jnp.where(at == 0, mis, jnp.where(at == 1, scl, 0.0))
    out_ref[:, :, 1152:1280] = jnp.broadcast_to(line[None], (out_ref.shape[0], 1, 128))


def finish_kernel(part_ref, crd_ref, new_ref):
    sums = jnp.sum(part_ref[...], axis=0)
    lines = [sums[:, 128 * k : 128 * k + 128] for k in range(9)]
    half = jnp.concatenate(lines[:8], axis=0)
    pull = jnp.concatenate([half[:, 0:64], half[:, 64:128]], axis=0)
    rate = lines[8][:, 0:64]
    wsum = lines[8][:, 64:128]
    crd = crd_ref[...]
    new_ref[...] = crd + (rate * crd - pull) / wsum


def stress_kernel(part_ref, out_ref):
    sums = jnp.sum(part_ref[...], axis=0)
    out_ref[...] = sums[:, 0:1] / sums[:, 1:2]


def column_moves(n_row, n_col, n_depth):
    moves = []
    for row in range(n_row):
        for at in range(n_col * n_depth):
            moves.append((row * n_col * n_depth + at, (at % n_row * n_col + row) * n_depth + at // n_row))
    return moves


def shards(embeddings, coords, pair_weight):
    rows, cols = pair_weight.shape
    points = embeddings.shape[1]
    group = rows // points
    n_row, n_z, n_core, n_depth = (lax.axis_size(a) for a in ("row", "z", "core", "depth"))
    likes = n_z * n_depth

    packed = pl.pallas_call(
        pack_kernel,
        out_shape=jax.ShapeDtypeStruct((points, LANES), BF16),
        name="pack",
    )(embeddings, coords)
    moves = column_moves(n_row, n_z * n_core, n_depth)
    moved = lax.ppermute(packed, ("row", "z", "core", "depth"), moves)
    copies = jnp.broadcast_to(packed[None], (likes, points, LANES))
    copies, moved = lax.optimization_barrier((copies, moved))
    own = lax.all_to_all(copies, ("z", "depth"), 0, 0, tiled=True)
    moved = jnp.broadcast_to(moved[None], (n_row, points, LANES))
    moved, own = lax.optimization_barrier((moved, own))
    own = own.reshape(rows // n_core, LANES)
    oth = lax.ppermute(own, "core", [(0, 1), (1, 0)])
    t_cols = lax.all_to_all(moved, "row", 0, 0, tiled=True).reshape(cols, LANES)

    vmem = pl.BlockSpec(memory_space=pltpu.VMEM)
    tm = 256
    parts = pl.pallas_call(
        pairs_kernel,
        in_specs=[
            vmem,
            vmem,
            vmem,
            pl.BlockSpec(memory_space=pltpu.HBM),
        ],
        out_specs=vmem,
        out_shape=jax.ShapeDtypeStruct((group, 1, 1280), F32),
        scratch_shapes=[
            pltpu.VMEM((rows, cols), BF16),
            pltpu.VMEM((LANES, cols), BF16),
            pltpu.VMEM((LANES, cols), BF16),
            pltpu.VMEM((48, cols), BF16),
            pltpu.VMEM((tm, cols), BF16),
            pltpu.VMEM((2, tm, cols), F32),
            pltpu.VMEM((2, tm, cols), F32),
            pltpu.SemaphoreType.DMA((rows // tm,)),
        ],
        compiler_params=pltpu.CompilerParams(vmem_limit_bytes=52 * 1024 * 1024),
        name="pairs",
    )(own, oth, t_cols, pair_weight)
    parts = lax.all_to_all(parts, ("z", "core", "depth"), 0, 0, tiled=True)
    shares = jnp.sum(parts[:, :, 1152:], axis=0, keepdims=True)
    shares = lax.all_to_all(jnp.broadcast_to(shares, (n_row, 1, 128)), "row", 0, 0, tiled=True)
    new_coords = pl.pallas_call(
        finish_kernel,
        out_shape=jax.ShapeDtypeStruct(coords.shape, F32),
        cost_estimate=pl.CostEstimate(flops=100000, bytes_accessed=200000, transcendentals=0),
        name="finish",
    )(parts, coords)
    stress = pl.pallas_call(
        stress_kernel,
        out_shape=jax.ShapeDtypeStruct((1, 1), F32),
        name="stress",
    )(shares)
    return (new_coords, stress[0, 0])


def solution(mesh):
    n_row, n_col, n_depth = (mesh.shape[a] for a in ("row", "col", "depth"))
    fine = jax.sharding.Mesh(
        mesh.devices.reshape(n_row, n_col // 2, 2, n_depth), ("row", "z", "core", "depth")
    )
    points = P(None, ("row", "z", "core", "depth"))
    return jax.shard_map(
        shards,
        mesh=fine,
        in_specs=(points, points, P("row", ("z", "core", "depth"))),
        out_specs=(points, P()),
        check_vma=False,
    )
```

```python
import jax
import jax.numpy as jnp
from jax import lax
from jax.experimental import pallas as pl
from jax.experimental.pallas import tpu as pltpu
from jax.sharding import PartitionSpec as P

F32 = jnp.float32
BF16 = jnp.bfloat16

EMB, XH, XL, XH2, QF, QX, ONE, LANES = 0, 64, 80, 96, 112, 115, 118, 128
TINY = 1e-30


def bilinear_form(kind):
    a = lax.broadcasted_iota(jnp.int32, (LANES, LANES), 0)
    b = lax.broadcasted_iota(jnp.int32, (LANES, LANES), 1)

    def band(first, count, shift):
        return (a >= first) & (a < first + count) & (b == a + shift)

    if kind == 0:
        cross = band(EMB, 64, 0)
        square, unit = QF, 1.0 / 64.0
    else:
        cross = band(XH, 16, 0) | band(XL, 16, XH2 - XL) | band(XH2, 16, XL - XH2)
        square, unit = QX, 1.0
    norms = band(square, 3, ONE - square) | band(ONE, 3, square - ONE)
    return jnp.where(cross, -2.0 * unit, jnp.where(norms, unit, 0.0)).astype(BF16)


def split3(value):
    hi = value.astype(BF16).astype(F32)
    mid = (value - hi).astype(BF16).astype(F32)
    low = (value - hi - mid).astype(BF16).astype(F32)
    return hi, mid, low


def pack_kernel(emb_ref, crd_ref, own_ref, out_ref):
    emb = emb_ref[...].astype(F32)
    crd = crd_ref[...]
    points = emb.shape[1]
    hi = crd.astype(BF16).astype(F32)
    low = (crd - hi).astype(BF16).astype(F32)
    squares = split3(jnp.sum(emb * emb, axis=0, keepdims=True))
    squares += split3(jnp.sum(crd * crd, axis=0, keepdims=True))
    lane = lax.broadcasted_iota(jnp.int32, (16, points), 0)
    tail = jnp.where((lane >= ONE - QF) & (lane < ONE - QF + 3), 1.0, 0.0)
    for k, sq in enumerate(squares):
        tail = jnp.where(lane == k, sq, tail)
    rows = jnp.concatenate([emb, hi, low, hi, tail], axis=0)
    mine = rows.T.astype(BF16)
    own_ref[...] = mine
    for k in range(out_ref.shape[0]):
        out_ref[k] = mine


def pairs_kernel(own_ref, oth_ref, col_ref, w_hbm, out_ref, w_ref, f_scr, x_scr, flat_scr, c_scr, f_tiles, x_tiles, sems):
    total_rows, total = w_ref.shape
    tm = c_scr.shape[0]
    tn = min(256, total)
    steps = total_rows // tm
    first = lax.axis_index("core") == 0

    def fetch(i):
        at = pl.ds(i * tm, tm)
        return pltpu.make_async_copy(w_hbm.at[at, :], w_ref.at[at, :], sems.at[i])

    for i in range(steps):
        fetch(i).start()
    all_cols = col_ref[...]
    last = (((1,), (1,)), ((), ()))
    form_f = bilinear_form(0)
    f_scr[...] = lax.dot_general(form_f, all_cols, last, preferred_element_type=F32).astype(BF16)
    x_scr[...] = lax.dot_general(bilinear_form(1), all_cols, last, preferred_element_type=F32).astype(BF16)
    a = lax.broadcasted_iota(jnp.int32, (LANES, LANES), 0)
    b = lax.broadcasted_iota(jnp.int32, (LANES, LANES), 1)
    same = jnp.where(a == b, 1.0, 0.0).astype(BF16)
    flat_scr[...] = lax.dot_general(same, all_cols, last, preferred_element_type=F32).astype(BF16)

    def row_block(i):
        pieces = []
        for k in range(tm // 256):
            cut = pl.ds(pl.multiple_of(i * (tm // 2) + k * 128, 128), 128)
            own, oth = own_ref[cut, :], oth_ref[cut, :]
            pieces += [jnp.where(first, own, oth), jnp.where(first, oth, own)]
        return jnp.concatenate(pieces, axis=0)

    def squares(rows, slot):
        f_tiles[slot] = jnp.dot(rows, f_scr[...], preferred_element_type=F32)
        x_tiles[slot] = jnp.dot(rows, x_scr[...], preferred_element_type=F32)

    def block(i, slot, mis, scl):
        fetch(i).wait()
        squares(row_block(jnp.minimum(i + 1, steps - 1)), 1 - slot)
        bent = lax.dot_general(form_f, row_block(i), last, preferred_element_type=F32)
        base = i * tm
        acc = jnp.zeros((48, tm), F32)
        wacc = jnp.zeros((LANES, tm), F32)
        for start in range(0, total, tn):
            cut = slice(start, start + tn)
            for r in range(0, tm, 16):
                f2 = jnp.maximum(f_tiles[slot, r : r + 16, cut], TINY)
                x2 = jnp.maximum(x_tiles[slot, r : r + 16, cut], TINY)
                wb = w_ref[pl.ds(pl.multiple_of(base + r, 16), 16), cut]
                dissim = f2 * lax.rsqrt(f2)
                inv = lax.rsqrt(x2)
                diff = dissim - x2 * inv
                c_scr[r : r + 16, cut] = wb * (dissim * jnp.minimum(inv, 1.0)).astype(BF16)
                miss = wb.astype(F32) * (diff * diff)
                mis += miss[0:8] + miss[8:16]
            wb = w_ref[pl.ds(pl.multiple_of(base, tm), tm), cut]
            picked = jnp.concatenate([flat_scr[XH : XH + 32, cut], flat_scr[QF:, cut]], axis=0)
            acc += lax.dot_general(picked, c_scr[:, cut], last, preferred_element_type=F32)
            wacc += lax.dot_general(flat_scr[:, cut], wb, last, preferred_element_type=F32)
        scl += jnp.sum((bent * wacc).reshape(LANES // 8, 8, tm), axis=0)
        less = acc[0:32] - wacc[XH : XH + 32]
        pull = less[0:16] + less[16:32]
        wsum = wacc[ONE : ONE + 1]
        rate = acc[32 + ONE - QF : 33 + ONE - QF] - wsum
        for k in range(tm // 64):
            cut = slice(64 * k, 64 * k + 64)
            to = i * (tm // 64) + k
            for j in range(8):
                line = jnp.concatenate([pull[j : j + 1, cut], pull[j + 8 : j + 9, cut]], axis=1)
                out_ref[to, :, 128 * j : 128 * j + 128] = line
            out_ref[to, :, 1024:1152] = jnp.concatenate([rate[:, cut], wsum[:, cut]], axis=1)
        return mis, scl

    def two(k, carry):
        carry = block(2 * k, 0, *carry)
        return block(2 * k + 1, 1, *carry)

    squares(row_block(0), 0)
    mis, scl = lax.fori_loop(
        0, steps // 2, two, (jnp.zeros((8, tn), F32), jnp.zeros((8, tm), F32))
    )
    if steps % 2:
        mis, scl = block(steps - 1, 0, mis, scl)
    mis = jnp.sum(jnp.sum(mis, axis=0, keepdims=True), axis=1, keepdims=True)
    scl = jnp.sum(jnp.sum(scl, axis=0, keepdims=True), axis=1, keepdims=True)
    at = lax.broadcasted_iota(jnp.int32, (1, 128), 1)
    line = jnp.where(at == 0, mis, jnp.where(at == 1, scl, 0.0))
    out_ref[:, :, 1152:1280] = jnp.broadcast_to(line[None], (out_ref.shape[0], 1, 128))


def finish_kernel(part_ref, crd_ref, new_ref):
    sums = jnp.sum(part_ref[...], axis=0)
    lines = [sums[:, 128 * k : 128 * k + 128] for k in range(9)]
    half = jnp.concatenate(lines[:8], axis=0)
    pull = jnp.concatenate([half[:, 0:64], half[:, 64:128]], axis=0)
    rate = lines[8][:, 0:64]
    wsum = lines[8][:, 64:128]
    crd = crd_ref[...]
    new_ref[...] = crd + (rate * crd - pull) / wsum


def stress_kernel(part_ref, out_ref):
    sums = jnp.sum(part_ref[...], axis=0)
    out_ref[...] = sums[:, 0:1] / sums[:, 1:2]


def column_moves(n_row, n_col, n_depth):
    moves = []
    for row in range(n_row):
        for at in range(n_col * n_depth):
            moves.append((row * n_col * n_depth + at, (at % n_row * n_col + row) * n_depth + at // n_row))
    return moves


def shards(embeddings, coords, pair_weight):
    rows, cols = pair_weight.shape
    points = embeddings.shape[1]
    group = rows // points
    n_row, n_z, n_core, n_depth = (lax.axis_size(a) for a in ("row", "z", "core", "depth"))
    likes = n_z * n_depth

    packed = pl.pallas_call(
        pack_kernel,
        out_shape=(
            jax.ShapeDtypeStruct((points, LANES), BF16),
            jax.ShapeDtypeStruct((likes, points, LANES), BF16),
        ),
        name="pack",
    )(embeddings, coords)
    moves = column_moves(n_row, n_z * n_core, n_depth)
    moved = lax.ppermute(packed[0], ("row", "z", "core", "depth"), moves)
    own = lax.all_to_all(packed[1], ("z", "depth"), 0, 0, tiled=True).reshape(rows // n_core, LANES)
    moved = jnp.broadcast_to(moved[None], (n_row, points, LANES))
    moved, own = lax.optimization_barrier((moved, own))
    oth = lax.ppermute(own, "core", [(0, 1), (1, 0)])
    t_cols = lax.all_to_all(moved, "row", 0, 0, tiled=True).reshape(cols, LANES)

    vmem = pl.BlockSpec(memory_space=pltpu.VMEM)
    tm = 256
    parts = pl.pallas_call(
        pairs_kernel,
        in_specs=[
            vmem,
            vmem,
            vmem,
            pl.BlockSpec(memory_space=pltpu.HBM),
        ],
        out_specs=vmem,
        out_shape=jax.ShapeDtypeStruct((group, 1, 1280), F32),
        scratch_shapes=[
            pltpu.VMEM((rows, cols), BF16),
            pltpu.VMEM((LANES, cols), BF16),
            pltpu.VMEM((LANES, cols), BF16),
            pltpu.VMEM((LANES, cols), BF16),
            pltpu.VMEM((tm, cols), BF16),
            pltpu.VMEM((2, tm, cols), F32),
            pltpu.VMEM((2, tm, cols), F32),
            pltpu.SemaphoreType.DMA((rows // tm,)),
        ],
        compiler_params=pltpu.CompilerParams(vmem_limit_bytes=52 * 1024 * 1024),
        name="pairs",
    )(own, oth, t_cols, pair_weight)
    parts = lax.all_to_all(parts, ("z", "core", "depth"), 0, 0, tiled=True)
    shares = jnp.sum(parts[:, :, 1152:], axis=0, keepdims=True)
    shares = lax.all_to_all(jnp.broadcast_to(shares, (n_row, 1, 128)), "row", 0, 0, tiled=True)
    new_coords = pl.pallas_call(
        finish_kernel,
        out_shape=jax.ShapeDtypeStruct(coords.shape, F32),
        cost_estimate=pl.CostEstimate(flops=100000, bytes_accessed=200000, transcendentals=0),
        name="finish",
    )(parts, coords)
    stress = pl.pallas_call(
        stress_kernel,
        out_shape=jax.ShapeDtypeStruct((1, 1), F32),
        name="stress",
    )(shares)
    return (new_coords, stress[0, 0])


def solution(mesh):
    n_row, n_col, n_depth = (mesh.shape[a] for a in ("row", "col", "depth"))
    fine = jax.sharding.Mesh(
        mesh.devices.reshape(n_row, n_col // 2, 2, n_depth), ("row", "z", "core", "depth")
    )
    points = P(None, ("row", "z", "core", "depth"))
    return jax.shard_map(
        shards,
        mesh=fine,
        in_specs=(points, points, P("row", ("z", "core", "depth"))),
        out_specs=(points, P()),
        check_vma=False,
    )
```

```python
import jax
import jax.numpy as jnp
from jax import lax
from jax.experimental import pallas as pl
from jax.experimental.pallas import tpu as pltpu
from jax.sharding import PartitionSpec as P

F32 = jnp.float32
BF16 = jnp.bfloat16

EMB, XH, XL, XH2, QF, QX, ONE, LANES = 0, 64, 80, 96, 112, 115, 118, 128
TINY = 1e-30


def bilinear_form(kind):
    a = lax.broadcasted_iota(jnp.int32, (LANES, LANES), 0)
    b = lax.broadcasted_iota(jnp.int32, (LANES, LANES), 1)

    def band(first, count, shift):
        return (a >= first) & (a < first + count) & (b == a + shift)

    if kind == 0:
        cross = band(EMB, 64, 0)
        square, unit = QF, 1.0 / 64.0
    else:
        cross = band(XH, 16, 0) | band(XL, 16, XH2 - XL) | band(XH2, 16, XL - XH2)
        square, unit = QX, 1.0
    norms = band(square, 3, ONE - square) | band(ONE, 3, square - ONE)
    return jnp.where(cross, -2.0 * unit, jnp.where(norms, unit, 0.0)).astype(BF16)


def split3(value):
    hi = value.astype(BF16).astype(F32)
    mid = (value - hi).astype(BF16).astype(F32)
    low = (value - hi - mid).astype(BF16).astype(F32)
    return hi, mid, low


def pack_kernel(emb_ref, crd_ref, own_ref, out_ref):
    emb = emb_ref[...].astype(F32)
    crd = crd_ref[...]
    points = emb.shape[1]
    hi = crd.astype(BF16).astype(F32)
    low = (crd - hi).astype(BF16).astype(F32)
    squares = split3(jnp.sum(emb * emb, axis=0, keepdims=True))
    squares += split3(jnp.sum(crd * crd, axis=0, keepdims=True))
    lane = lax.broadcasted_iota(jnp.int32, (16, points), 0)
    tail = jnp.where((lane >= ONE - QF) & (lane < ONE - QF + 3), 1.0, 0.0)
    for k, sq in enumerate(squares):
        tail = jnp.where(lane == k, sq, tail)
    rows = jnp.concatenate([emb, hi, low, hi, tail], axis=0)
    mine = rows.T.astype(BF16)
    own_ref[...] = mine
    for k in range(out_ref.shape[0]):
        out_ref[k] = mine


def pairs_kernel(own_ref, oth_ref, col_ref, w_hbm, out_ref, w_ref, f_scr, x_scr, flat_scr, c_scr, f_tiles, x_tiles, sems):
    total_rows, total = w_ref.shape
    tm = c_scr.shape[0]
    tn = min(256, total)
    steps = total_rows // tm
    first = lax.axis_index("core") == 0

    def fetch(i):
        at = pl.ds(i * tm, tm)
        return pltpu.make_async_copy(w_hbm.at[at, :], w_ref.at[at, :], sems.at[i])

    for i in range(steps):
        fetch(i).start()
    all_cols = col_ref[...]
    last = (((1,), (1,)), ((), ()))
    form_f = bilinear_form(0)
    f_scr[...] = lax.dot_general(form_f, all_cols, last, preferred_element_type=F32).astype(BF16)
    x_scr[...] = lax.dot_general(bilinear_form(1), all_cols, last, preferred_element_type=F32).astype(BF16)
    a = lax.broadcasted_iota(jnp.int32, (LANES, LANES), 0)
    b = lax.broadcasted_iota(jnp.int32, (LANES, LANES), 1)
    same = jnp.where(a == b, 1.0, 0.0).astype(BF16)
    flat_scr[...] = lax.dot_general(same, all_cols, last, preferred_element_type=F32).astype(BF16)

    def row_block(i):
        pieces = []
        for k in range(tm // 256):
            cut = pl.ds(pl.multiple_of(i * (tm // 2) + k * 128, 128), 128)
            own, oth = own_ref[cut, :], oth_ref[cut, :]
            pieces += [jnp.where(first, own, oth), jnp.where(first, oth, own)]
        return jnp.concatenate(pieces, axis=0)

    def squares(rows, slot):
        f_tiles[slot] = jnp.dot(rows, f_scr[...], preferred_element_type=F32)
        x_tiles[slot] = jnp.dot(rows, x_scr[...], preferred_element_type=F32)

    def block(i, slot, mis, scl, more=True):
        fetch(i).wait()
        if more:
            squares(row_block(i + 1), 1 - slot)
        bent = lax.dot_general(form_f, row_block(i), last, preferred_element_type=F32)
        base = i * tm
        acc = jnp.zeros((48, tm), F32)
        wacc = jnp.zeros((LANES, tm), F32)
        for start in range(0, total, tn):
            cut = slice(start, start + tn)
            for r in range(0, tm, 32):
                f2 = jnp.maximum(f_tiles[slot, r : r + 32, cut], TINY)
                x2 = jnp.maximum(x_tiles[slot, r : r + 32, cut], TINY)
                w = w_ref[pl.ds(pl.multiple_of(base + r, 32), 32), cut].astype(F32)
                dissim = f2 * lax.rsqrt(f2)
                inv = lax.rsqrt(x2)
                diff = dissim - x2 * inv
                c_scr[r : r + 32, cut] = (w * (dissim * jnp.minimum(inv, 1.0))).astype(BF16)
                miss = w * (diff * diff)
                mis += (miss[0:8] + miss[8:16]) + (miss[16:24] + miss[24:32])
            wb = w_ref[pl.ds(pl.multiple_of(base, tm), tm), cut]
            picked = jnp.concatenate([flat_scr[XH : XH + 32, cut], flat_scr[QF:, cut]], axis=0)
            acc += lax.dot_general(picked, c_scr[:, cut], last, preferred_element_type=F32)
            wacc += lax.dot_general(flat_scr[:, cut], wb, last, preferred_element_type=F32)
        scl += jnp.sum((bent * wacc).reshape(LANES // 8, 8, tm), axis=0)
        less = acc[0:32] - wacc[XH : XH + 32]
        pull = less[0:16] + less[16:32]
        wsum = wacc[ONE : ONE + 1]
        rate = acc[32 + ONE - QF : 33 + ONE - QF] - wsum
        for k in range(tm // 64):
            cut = slice(64 * k, 64 * k + 64)
            to = i * (tm // 64) + k
            for j in range(8):
                line = jnp.concatenate([pull[j : j + 1, cut], pull[j + 8 : j + 9, cut]], axis=1)
                out_ref[to, :, 128 * j : 128 * j + 128] = line
            out_ref[to, :, 1024:1152] = jnp.concatenate([rate[:, cut], wsum[:, cut]], axis=1)
        return mis, scl

    def two(k, carry):
        carry = block(2 * k, 0, *carry)
        return block(2 * k + 1, 1, *carry)

    squares(row_block(0), 0)
    pairs = (steps - 1) // 2
    sums = lax.fori_loop(0, pairs, two, (jnp.zeros((8, tn), F32), jnp.zeros((8, tm), F32)))
    for i in range(2 * pairs, steps):
        sums = block(i, i % 2, *sums, more=i + 1 < steps)
    mis, scl = sums
    mis = jnp.sum(jnp.sum(mis, axis=0, keepdims=True), axis=1, keepdims=True)
    scl = jnp.sum(jnp.sum(scl, axis=0, keepdims=True), axis=1, keepdims=True)
    at = lax.broadcasted_iota(jnp.int32, (1, 128), 1)
    line = jnp.where(at == 0, mis, jnp.where(at == 1, scl, 0.0))
    out_ref[:, :, 1152:1280] = jnp.broadcast_to(line[None], (out_ref.shape[0], 1, 128))


def finish_kernel(part_ref, crd_ref, new_ref):
    sums = jnp.sum(part_ref[...], axis=0)
    lines = [sums[:, 128 * k : 128 * k + 128] for k in range(9)]
    half = jnp.concatenate(lines[:8], axis=0)
    pull = jnp.concatenate([half[:, 0:64], half[:, 64:128]], axis=0)
    rate = lines[8][:, 0:64]
    wsum = lines[8][:, 64:128]
    crd = crd_ref[...]
    new_ref[...] = crd + (rate * crd - pull) / wsum


def stress_kernel(part_ref, out_ref):
    sums = jnp.sum(part_ref[...], axis=0)
    out_ref[...] = sums[:, 0:1] / sums[:, 1:2]


def column_moves(n_row, n_col, n_depth):
    moves = []
    for row in range(n_row):
        for at in range(n_col * n_depth):
            moves.append((row * n_col * n_depth + at, (at % n_row * n_col + row) * n_depth + at // n_row))
    return moves


def shards(embeddings, coords, pair_weight):
    rows, cols = pair_weight.shape
    points = embeddings.shape[1]
    group = rows // points
    n_row, n_z, n_core, n_depth = (lax.axis_size(a) for a in ("row", "z", "core", "depth"))
    likes = n_z * n_depth

    packed = pl.pallas_call(
        pack_kernel,
        out_shape=(
            jax.ShapeDtypeStruct((points, LANES), BF16),
            jax.ShapeDtypeStruct((likes, points, LANES), BF16),
        ),
        name="pack",
    )(embeddings, coords)
    moves = column_moves(n_row, n_z * n_core, n_depth)
    moved = lax.ppermute(packed[0], ("row", "z", "core", "depth"), moves)
    own = lax.all_to_all(packed[1], ("z", "depth"), 0, 0, tiled=True).reshape(rows // n_core, LANES)
    moved = jnp.broadcast_to(moved[None], (n_row, points, LANES))
    moved, own = lax.optimization_barrier((moved, own))
    oth = lax.ppermute(own, "core", [(0, 1), (1, 0)])
    t_cols = lax.all_to_all(moved, "row", 0, 0, tiled=True).reshape(cols, LANES)

    vmem = pl.BlockSpec(memory_space=pltpu.VMEM)
    tm = 256
    parts = pl.pallas_call(
        pairs_kernel,
        in_specs=[
            vmem,
            vmem,
            vmem,
            pl.BlockSpec(memory_space=pltpu.HBM),
        ],
        out_specs=vmem,
        out_shape=jax.ShapeDtypeStruct((group, 1, 1280), F32),
        scratch_shapes=[
            pltpu.VMEM((rows, cols), BF16),
            pltpu.VMEM((LANES, cols), BF16),
            pltpu.VMEM((LANES, cols), BF16),
            pltpu.VMEM((LANES, cols), BF16),
            pltpu.VMEM((tm, cols), BF16),
            pltpu.VMEM((2, tm, cols), F32),
            pltpu.VMEM((2, tm, cols), F32),
            pltpu.SemaphoreType.DMA((rows // tm,)),
        ],
        compiler_params=pltpu.CompilerParams(vmem_limit_bytes=52 * 1024 * 1024),
        name="pairs",
    )(own, oth, t_cols, pair_weight)
    parts = lax.all_to_all(parts, ("z", "core", "depth"), 0, 0, tiled=True)
    shares = jnp.sum(parts[:, :, 1152:], axis=0, keepdims=True)
    shares = lax.all_to_all(jnp.broadcast_to(shares, (n_row, 1, 128)), "row", 0, 0, tiled=True)
    new_coords = pl.pallas_call(
        finish_kernel,
        out_shape=jax.ShapeDtypeStruct(coords.shape, F32),
        cost_estimate=pl.CostEstimate(flops=100000, bytes_accessed=200000, transcendentals=0),
        name="finish",
    )(parts, coords)
    stress = pl.pallas_call(
        stress_kernel,
        out_shape=jax.ShapeDtypeStruct((1, 1), F32),
        name="stress",
    )(shares)
    return (new_coords, stress[0, 0])


def solution(mesh):
    n_row, n_col, n_depth = (mesh.shape[a] for a in ("row", "col", "depth"))
    fine = jax.sharding.Mesh(
        mesh.devices.reshape(n_row, n_col // 2, 2, n_depth), ("row", "z", "core", "depth")
    )
    points = P(None, ("row", "z", "core", "depth"))
    return jax.shard_map(
        shards,
        mesh=fine,
        in_specs=(points, points, P("row", ("z", "core", "depth"))),
        out_specs=(points, P()),
        check_vma=False,
    )
```

```python
import jax
import jax.numpy as jnp
from jax import lax
from jax.experimental import pallas as pl
from jax.experimental.pallas import tpu as pltpu
from jax.sharding import PartitionSpec as P

F32 = jnp.float32
BF16 = jnp.bfloat16

EMB, XH, XL, XH2, QF, QX, ONE, LANES = 0, 64, 80, 96, 112, 115, 118, 128
TINY = 1e-30


def bilinear_form(kind):
    a = lax.broadcasted_iota(jnp.int32, (LANES, LANES), 0)
    b = lax.broadcasted_iota(jnp.int32, (LANES, LANES), 1)

    def band(first, count, shift):
        return (a >= first) & (a < first + count) & (b == a + shift)

    if kind == 0:
        cross = band(EMB, 64, 0)
        square, unit = QF, 1.0 / 64.0
    else:
        cross = band(XH, 16, 0) | band(XL, 16, XH2 - XL) | band(XH2, 16, XL - XH2)
        square, unit = QX, 1.0
    norms = band(square, 3, ONE - square) | band(ONE, 3, square - ONE)
    return jnp.where(cross, -2.0 * unit, jnp.where(norms, unit, 0.0)).astype(BF16)


def split3(value):
    hi = value.astype(BF16).astype(F32)
    mid = (value - hi).astype(BF16).astype(F32)
    low = (value - hi - mid).astype(BF16).astype(F32)
    return hi, mid, low


def pack_kernel(emb_ref, crd_ref, own_ref, out_ref):
    emb = emb_ref[...].astype(F32)
    crd = crd_ref[...]
    points = emb.shape[1]
    hi = crd.astype(BF16).astype(F32)
    low = (crd - hi).astype(BF16).astype(F32)
    squares = split3(jnp.sum(emb * emb, axis=0, keepdims=True))
    squares += split3(jnp.sum(crd * crd, axis=0, keepdims=True))
    lane = lax.broadcasted_iota(jnp.int32, (16, points), 0)
    tail = jnp.where((lane >= ONE - QF) & (lane < ONE - QF + 3), 1.0, 0.0)
    for k, sq in enumerate(squares):
        tail = jnp.where(lane == k, sq, tail)
    rows = jnp.concatenate([emb, hi, low, hi, tail], axis=0)
    mine = rows.T.astype(BF16)
    own_ref[...] = mine
    for k in range(out_ref.shape[0]):
        out_ref[k] = mine


def spread_kernel(own_ref, out_ref):
    own = own_ref[...]
    for k in range(out_ref.shape[0]):
        out_ref[k] = own


def pairs_kernel(own_ref, oth_ref, col_ref, w_hbm, out_ref, w_ref, f_scr, x_scr, flat_scr, c_scr, f_tiles, x_tiles, sems):
    total_rows, total = w_ref.shape
    tm = c_scr.shape[1]
    tn = min(256, total)
    steps = total_rows // tm
    first = lax.axis_index("core") == 0

    def fetch(i):
        at = pl.ds(i * tm, tm)
        return pltpu.make_async_copy(w_hbm.at[at, :], w_ref.at[at, :], sems.at[i])

    for i in range(steps):
        fetch(i).start()
    all_cols = col_ref[...]
    last = (((1,), (1,)), ((), ()))
    form_f = bilinear_form(0)
    f_scr[...] = lax.dot_general(form_f, all_cols, last, preferred_element_type=F32).astype(BF16)
    x_scr[...] = lax.dot_general(bilinear_form(1), all_cols, last, preferred_element_type=F32).astype(BF16)
    a = lax.broadcasted_iota(jnp.int32, (LANES, LANES), 0)
    b = lax.broadcasted_iota(jnp.int32, (LANES, LANES), 1)
    same = jnp.where(a == b, 1.0, 0.0).astype(BF16)
    flat_scr[...] = lax.dot_general(same, all_cols, last, preferred_element_type=F32).astype(BF16)

    def row_block(i):
        pieces = []
        for k in range(tm // 256):
            cut = pl.ds(pl.multiple_of(i * (tm // 2) + k * 128, 128), 128)
            own, oth = own_ref[cut, :], oth_ref[cut, :]
            pieces += [jnp.where(first, own, oth), jnp.where(first, oth, own)]
        return jnp.concatenate(pieces, axis=0)

    def squares(rows, slot):
        f_tiles[slot] = jnp.dot(rows, f_scr[...], preferred_element_type=F32)
        x_tiles[slot] = jnp.dot(rows, x_scr[...], preferred_element_type=F32)

    def chain(i, slot, mis):
        base = i * tm
        for start in range(0, total, tn):
            cut = slice(start, start + tn)
            for r in range(0, tm, 32):
                f2 = jnp.maximum(f_tiles[slot, r : r + 32, cut], TINY)
                x2 = jnp.maximum(x_tiles[slot, r : r + 32, cut], TINY)
                w = w_ref[pl.ds(pl.multiple_of(base + r, 32), 32), cut].astype(F32)
                dissim = f2 * lax.rsqrt(f2)
                inv = lax.rsqrt(x2)
                diff = dissim - x2 * inv
                c_scr[slot, r : r + 32, cut] = (w * (dissim * jnp.minimum(inv, 1.0))).astype(BF16)
                miss = w * (diff * diff)
                mis += (miss[0:8] + miss[8:16]) + (miss[16:24] + miss[24:32])
        return mis

    def sums_of(i, slot, scl):
        rows = row_block(i)
        bent = lax.dot_general(form_f, rows, last, preferred_element_type=F32)
        picked = jnp.concatenate([flat_scr[XH : XH + 32, :], flat_scr[QF:, :]], axis=0)
        acc = lax.dot_general(picked, c_scr[slot], last, preferred_element_type=F32)
        wb = w_ref[pl.ds(pl.multiple_of(i * tm, tm), tm), :]
        wacc = lax.dot_general(flat_scr[...], wb, last, preferred_element_type=F32)
        scl += jnp.sum((bent * wacc).reshape(LANES // 8, 8, tm), axis=0)
        less = acc[0:32] - wacc[XH : XH + 32]
        pull = less[0:16] + less[16:32]
        wsum = wacc[ONE : ONE + 1]
        rate = acc[32 + ONE - QF : 33 + ONE - QF] - wsum
        for k in range(tm // 64):
            cut = slice(64 * k, 64 * k + 64)
            to = i * (tm // 64) + k
            for j in range(8):
                line = jnp.concatenate([pull[j : j + 1, cut], pull[j + 8 : j + 9, cut]], axis=1)
                out_ref[to, :, 128 * j : 128 * j + 128] = line
            out_ref[to, :, 1024:1152] = jnp.concatenate([rate[:, cut], wsum[:, cut]], axis=1)
        return scl

    def stage(i, slot, mis, scl, ahead=True, behind=True):
        fetch(i).wait()
        if ahead:
            squares(row_block(i + 1), 1 - slot)
        if behind:
            scl = sums_of(i - 1, 1 - slot, scl)
        return chain(i, slot, mis), scl

    def two(k, carry):
        carry = stage(2 * k + 1, 1, *carry)
        return stage(2 * k + 2, 0, *carry)

    squares(row_block(0), 0)
    carry = (jnp.zeros((8, tn), F32), jnp.zeros((8, tm), F32))
    carry = stage(0, 0, *carry, ahead=steps > 1, behind=False)
    loops = max(0, (steps - 2) // 2)
    carry = lax.fori_loop(0, loops, two, carry)
    for i in range(2 * loops + 1, steps):
        carry = stage(i, i % 2, *carry, ahead=i + 1 < steps)
    mis, scl = carry
    scl = sums_of(steps - 1, (steps - 1) % 2, scl)
    mis = jnp.sum(jnp.sum(mis, axis=0, keepdims=True), axis=1, keepdims=True)
    scl = jnp.sum(jnp.sum(scl, axis=0, keepdims=True), axis=1, keepdims=True)
    at = lax.broadcasted_iota(jnp.int32, (1, 128), 1)
    line = jnp.where(at == 0, mis, jnp.where(at == 1, scl, 0.0))
    out_ref[:, :, 1152:1280] = jnp.broadcast_to(line[None], (out_ref.shape[0], 1, 128))


def finish_kernel(part_ref, crd_ref, new_ref):
    sums = jnp.sum(part_ref[...], axis=0)
    lines = [sums[:, 128 * k : 128 * k + 128] for k in range(9)]
    half = jnp.concatenate(lines[:8], axis=0)
    pull = jnp.concatenate([half[:, 0:64], half[:, 64:128]], axis=0)
    rate = lines[8][:, 0:64]
    wsum = lines[8][:, 64:128]
    crd = crd_ref[...]
    new_ref[...] = crd + (rate * crd - pull) / wsum


def stress_kernel(part_ref, out_ref):
    sums = jnp.sum(part_ref[...], axis=0)
    out_ref[...] = sums[:, 0:1] / sums[:, 1:2]


def column_moves(n_row, n_col, n_depth):
    moves = []
    for row in range(n_row):
        for at in range(n_col * n_depth):
            moves.append((row * n_col * n_depth + at, (at % n_row * n_col + row) * n_depth + at // n_row))
    return moves


def shards(embeddings, coords, pair_weight):
    rows, cols = pair_weight.shape
    points = embeddings.shape[1]
    group = rows // points
    n_row, n_z, n_core, n_depth = (lax.axis_size(a) for a in ("row", "z", "core", "depth"))
    likes = n_z * n_depth

    packed = pl.pallas_call(
        pack_kernel,
        out_shape=(
            jax.ShapeDtypeStruct((points, LANES), BF16),
            jax.ShapeDtypeStruct((likes, points, LANES), BF16),
        ),
        name="pack",
    )(embeddings, coords)
    moves = column_moves(n_row, n_z * n_core, n_depth)
    moved = lax.ppermute(packed[0], ("row", "z", "core", "depth"), moves)
    own = lax.all_to_all(packed[1], ("z", "depth"), 0, 0, tiled=True).reshape(rows // n_core, LANES)
    moved = pl.pallas_call(
        spread_kernel,
        out_shape=jax.ShapeDtypeStruct((n_row, points, LANES), BF16),
        cost_estimate=pl.CostEstimate(flops=10**10, bytes_accessed=10**8, transcendentals=0),
        name="spread",
    )(moved)
    moved, own = lax.optimization_barrier((moved, own))
    oth = lax.ppermute(own, "core", [(0, 1), (1, 0)])
    t_cols = lax.all_to_all(moved, "row", 0, 0, tiled=True).reshape(cols, LANES)

    vmem = pl.BlockSpec(memory_space=pltpu.VMEM)
    tm = 256
    parts = pl.pallas_call(
        pairs_kernel,
        in_specs=[
            vmem,
            vmem,
            vmem,
            pl.BlockSpec(memory_space=pltpu.HBM),
        ],
        out_specs=vmem,
        out_shape=jax.ShapeDtypeStruct((group, 1, 1280), F32),
        scratch_shapes=[
            pltpu.VMEM((rows, cols), BF16),
            pltpu.VMEM((LANES, cols), BF16),
            pltpu.VMEM((LANES, cols), BF16),
            pltpu.VMEM((LANES, cols), BF16),
            pltpu.VMEM((2, tm, cols), BF16),
            pltpu.VMEM((2, tm, cols), F32),
            pltpu.VMEM((2, tm, cols), F32),
            pltpu.SemaphoreType.DMA((rows // tm,)),
        ],
        compiler_params=pltpu.CompilerParams(vmem_limit_bytes=52 * 1024 * 1024),
        name="pairs",
    )(own, oth, t_cols, pair_weight)
    parts = lax.all_to_all(parts, ("z", "core", "depth"), 0, 0, tiled=True)
    shares = jnp.sum(parts[:, :, 1152:], axis=0, keepdims=True)
    shares = lax.all_to_all(jnp.broadcast_to(shares, (n_row, 1, 128)), "row", 0, 0, tiled=True)
    new_coords = pl.pallas_call(
        finish_kernel,
        out_shape=jax.ShapeDtypeStruct(coords.shape, F32),
        cost_estimate=pl.CostEstimate(flops=100000, bytes_accessed=200000, transcendentals=0),
        name="finish",
    )(parts, coords)
    stress = pl.pallas_call(
        stress_kernel,
        out_shape=jax.ShapeDtypeStruct((1, 1), F32),
        name="stress",
    )(shares)
    return (new_coords, stress[0, 0])


def solution(mesh):
    n_row, n_col, n_depth = (mesh.shape[a] for a in ("row", "col", "depth"))
    fine = jax.sharding.Mesh(
        mesh.devices.reshape(n_row, n_col // 2, 2, n_depth), ("row", "z", "core", "depth")
    )
    points = P(None, ("row", "z", "core", "depth"))
    return jax.shard_map(
        shards,
        mesh=fine,
        in_specs=(points, points, P("row", ("z", "core", "depth"))),
        out_specs=(points, P()),
        check_vma=False,
    )
```

```python
import jax
import jax.numpy as jnp
from jax import lax
from jax.experimental import pallas as pl
from jax.experimental.pallas import tpu as pltpu
from jax.sharding import PartitionSpec as P

F32 = jnp.float32
BF16 = jnp.bfloat16

EMB, XH, XL, XH2, QF, QX, ONE, LANES = 0, 64, 80, 96, 112, 115, 118, 128
TINY = 1e-30


def bilinear_form(kind):
    a = lax.broadcasted_iota(jnp.int32, (LANES, LANES), 0)
    b = lax.broadcasted_iota(jnp.int32, (LANES, LANES), 1)

    def band(first, count, shift):
        return (a >= first) & (a < first + count) & (b == a + shift)

    if kind == 0:
        cross = band(EMB, 64, 0)
        square, unit = QF, 1.0 / 64.0
    else:
        cross = band(XH, 16, 0) | band(XL, 16, XH2 - XL) | band(XH2, 16, XL - XH2)
        square, unit = QX, 1.0
    norms = band(square, 3, ONE - square) | band(ONE, 3, square - ONE)
    return jnp.where(cross, -2.0 * unit, jnp.where(norms, unit, 0.0)).astype(BF16)


def split3(value):
    hi = value.astype(BF16).astype(F32)
    mid = (value - hi).astype(BF16).astype(F32)
    low = (value - hi - mid).astype(BF16).astype(F32)
    return hi, mid, low


def pack_kernel(emb_ref, crd_ref, own_ref, out_ref):
    emb = emb_ref[...].astype(F32)
    crd = crd_ref[...]
    hi = crd.astype(BF16).astype(F32)
    feats = jnp.concatenate([emb, hi, crd - hi], axis=0)
    half = feats.shape[0] // 2
    mine = jnp.concatenate([feats[:half], feats[half:]], axis=1).astype(BF16)
    own_ref[...] = mine
    for k in range(out_ref.shape[0]):
        out_ref[k] = mine


def unpack(shards):
    top, low = [], []
    for sh in shards:
        sh = sh.astype(F32)
        top.append(sh[:, 0:64])
        low.append(sh[:, 64:128])
    feats = jnp.concatenate([jnp.concatenate(top, axis=1), jnp.concatenate(low, axis=1)], axis=0)
    emb, hi, low = feats[0:64], feats[XH : XH + 16], feats[XL : XL + 16]
    crd = hi + low
    squares = split3(jnp.sum(emb * emb, axis=0, keepdims=True))
    squares += split3(jnp.sum(crd * crd, axis=0, keepdims=True))
    at = lax.broadcasted_iota(jnp.int32, (16, feats.shape[1]), 0)
    tail = jnp.where((at >= ONE - QF) & (at < ONE - QF + 3), 1.0, 0.0)
    for k, sq in enumerate(squares):
        tail = jnp.where(at == k, sq, tail)
    return jnp.concatenate([feats, hi, tail], axis=0)


def spread_kernel(own_ref, out_ref):
    own = own_ref[...]
    for k in range(out_ref.shape[0]):
        out_ref[k] = own


def pairs_kernel(own_ref, oth_ref, col_ref, w_hbm, out_ref, w_ref, f_scr, x_scr, flat_scr, rows_scr, c_scr, f_tiles, x_tiles, sems):
    total_rows, total = w_ref.shape
    tm = c_scr.shape[0]
    tn = min(256, total)
    steps = total_rows // tm
    first = lax.axis_index("core") == 0

    def fetch(i):
        at = pl.ds(i * tm, tm)
        return pltpu.make_async_copy(w_hbm.at[at, :], w_ref.at[at, :], sems.at[i])

    for i in range(steps):
        fetch(i).start()
    last = (((1,), (1,)), ((), ()))
    form_f = bilinear_form(0)
    form_x = bilinear_form(1)
    for s in range(0, col_ref.shape[0], 4):
        some = unpack([col_ref[k] for k in range(s, min(s + 4, col_ref.shape[0]))]).astype(BF16)
        cut = slice(64 * s, 64 * s + some.shape[1])
        flat_scr[:, cut] = some
        f_scr[:, cut] = jnp.dot(form_f, some, preferred_element_type=F32).astype(BF16)
        x_scr[:, cut] = jnp.dot(form_x, some, preferred_element_type=F32).astype(BF16)

    def squares(i, slot):
        shards = []
        for k in range(tm // 256):
            at = i * (tm // 128) + 2 * k
            own = [own_ref[at], own_ref[at + 1]]
            oth = [oth_ref[at], oth_ref[at + 1]]
            shards += [jnp.where(first, a, b) for a, b in zip(own, oth)]
            shards += [jnp.where(first, b, a) for a, b in zip(own, oth)]
        feats = unpack(shards)
        rows_scr[slot] = feats.astype(BF16)
        rows = feats.T.astype(BF16)
        f_tiles[slot] = jnp.dot(rows, f_scr[...], preferred_element_type=F32)
        x_tiles[slot] = jnp.dot(rows, x_scr[...], preferred_element_type=F32)

    def block(i, slot, mis, scl, more=True):
        fetch(i).wait()
        if more:
            squares(i + 1, 1 - slot)
        bent = jnp.dot(form_f, rows_scr[slot], preferred_element_type=F32)
        base = i * tm
        acc = jnp.zeros((48, tm), F32)
        wacc = jnp.zeros((LANES, tm), F32)
        for start in range(0, total, tn):
            cut = slice(start, start + tn)
            for r in range(0, tm, 32):
                f2 = jnp.maximum(f_tiles[slot, r : r + 32, cut], TINY)
                x2 = jnp.maximum(x_tiles[slot, r : r + 32, cut], TINY)
                w = w_ref[pl.ds(pl.multiple_of(base + r, 32), 32), cut].astype(F32)
                dissim = f2 * lax.rsqrt(f2)
                inv = lax.rsqrt(x2)
                diff = dissim - x2 * inv
                c_scr[r : r + 32, cut] = (w * (dissim * jnp.minimum(inv, 1.0))).astype(BF16)
                miss = w * (diff * diff)
                mis += (miss[0:8] + miss[8:16]) + (miss[16:24] + miss[24:32])
            wb = w_ref[pl.ds(pl.multiple_of(base, tm), tm), cut]
            picked = jnp.concatenate([flat_scr[XH : XH + 32, cut], flat_scr[QF:, cut]], axis=0)
            acc += lax.dot_general(picked, c_scr[:, cut], last, preferred_element_type=F32)
            wacc += lax.dot_general(flat_scr[:, cut], wb, last, preferred_element_type=F32)
        scl += jnp.sum((bent * wacc).reshape(LANES // 8, 8, tm), axis=0)
        less = acc[0:32] - wacc[XH : XH + 32]
        pull = less[0:16] + less[16:32]
        wsum = wacc[ONE : ONE + 1]
        rate = acc[32 + ONE - QF : 33 + ONE - QF] - wsum
        for k in range(tm // 64):
            cut = slice(64 * k, 64 * k + 64)
            to = i * (tm // 64) + k
            for j in range(8):
                line = jnp.concatenate([pull[j : j + 1, cut], pull[j + 8 : j + 9, cut]], axis=1)
                out_ref[to, :, 128 * j : 128 * j + 128] = line
            out_ref[to, :, 1024:1152] = jnp.concatenate([rate[:, cut], wsum[:, cut]], axis=1)
        return mis, scl

    def two(k, carry):
        carry = block(2 * k, 0, *carry)
        return block(2 * k + 1, 1, *carry)

    squares(0, 0)
    pairs = (steps - 1) // 2
    sums = lax.fori_loop(0, pairs, two, (jnp.zeros((8, tn), F32), jnp.zeros((8, tm), F32)))
    for i in range(2 * pairs, steps):
        sums = block(i, i % 2, *sums, more=i + 1 < steps)
    mis, scl = sums
    mis = jnp.sum(jnp.sum(mis, axis=0, keepdims=True), axis=1, keepdims=True)
    scl = jnp.sum(jnp.sum(scl, axis=0, keepdims=True), axis=1, keepdims=True)
    at = lax.broadcasted_iota(jnp.int32, (1, 128), 1)
    line = jnp.where(at == 0, mis, jnp.where(at == 1, scl, 0.0))
    out_ref[:, :, 1152:1280] = jnp.broadcast_to(line[None], (out_ref.shape[0], 1, 128))


def finish_kernel(part_ref, crd_ref, new_ref):
    sums = jnp.sum(part_ref[...], axis=0)
    lines = [sums[:, 128 * k : 128 * k + 128] for k in range(9)]
    half = jnp.concatenate(lines[:8], axis=0)
    pull = jnp.concatenate([half[:, 0:64], half[:, 64:128]], axis=0)
    rate = lines[8][:, 0:64]
    wsum = lines[8][:, 64:128]
    crd = crd_ref[...]
    new_ref[...] = crd + (rate * crd - pull) / wsum


def stress_kernel(part_ref, out_ref):
    sums = jnp.sum(part_ref[...], axis=0)
    out_ref[...] = sums[:, 0:1] / sums[:, 1:2]


def column_moves(n_row, n_col, n_depth):
    moves = []
    for row in range(n_row):
        for at in range(n_col * n_depth):
            moves.append((row * n_col * n_depth + at, (at % n_row * n_col + row) * n_depth + at // n_row))
    return moves


def shards(embeddings, coords, pair_weight):
    rows, cols = pair_weight.shape
    points = embeddings.shape[1]
    group = rows // points
    n_row, n_z, n_core, n_depth = (lax.axis_size(a) for a in ("row", "z", "core", "depth"))
    likes = n_z * n_depth

    shard = (48, 128)
    packed = pl.pallas_call(
        pack_kernel,
        out_shape=(
            jax.ShapeDtypeStruct(shard, BF16),
            jax.ShapeDtypeStruct((likes,) + shard, BF16),
        ),
        name="pack",
    )(embeddings, coords)
    moves = column_moves(n_row, n_z * n_core, n_depth)
    moved = lax.ppermute(packed[0], ("row", "z", "core", "depth"), moves)
    own = lax.all_to_all(packed[1], ("z", "depth"), 0, 0, tiled=True)
    moved = pl.pallas_call(
        spread_kernel,
        out_shape=jax.ShapeDtypeStruct((n_row,) + shard, BF16),
        cost_estimate=pl.CostEstimate(flops=10**10, bytes_accessed=10**8, transcendentals=0),
        name="spread",
    )(moved)
    moved, own = lax.optimization_barrier((moved, own))
    oth = lax.ppermute(own, "core", [(0, 1), (1, 0)])
    t_cols = lax.all_to_all(moved, "row", 0, 0, tiled=True)

    vmem = pl.BlockSpec(memory_space=pltpu.VMEM)
    tm = 256
    parts = pl.pallas_call(
        pairs_kernel,
        in_specs=[
            vmem,
            vmem,
            vmem,
            pl.BlockSpec(memory_space=pltpu.HBM),
        ],
        out_specs=vmem,
        out_shape=jax.ShapeDtypeStruct((group, 1, 1280), F32),
        scratch_shapes=[
            pltpu.VMEM((rows, cols), BF16),
            pltpu.VMEM((LANES, cols), BF16),
            pltpu.VMEM((LANES, cols), BF16),
            pltpu.VMEM((LANES, cols), BF16),
            pltpu.VMEM((2, LANES, tm), BF16),
            pltpu.VMEM((tm, cols), BF16),
            pltpu.VMEM((2, tm, cols), F32),
            pltpu.VMEM((2, tm, cols), F32),
            pltpu.SemaphoreType.DMA((rows // tm,)),
        ],
        compiler_params=pltpu.CompilerParams(vmem_limit_bytes=52 * 1024 * 1024),
        name="pairs",
    )(own, oth, t_cols, pair_weight)
    parts = lax.all_to_all(parts, ("z", "core", "depth"), 0, 0, tiled=True)
    shares = jnp.sum(parts[:, :, 1152:], axis=0, keepdims=True)
    shares = lax.all_to_all(jnp.broadcast_to(shares, (n_row, 1, 128)), "row", 0, 0, tiled=True)
    new_coords = pl.pallas_call(
        finish_kernel,
        out_shape=jax.ShapeDtypeStruct(coords.shape, F32),
        cost_estimate=pl.CostEstimate(flops=100000, bytes_accessed=200000, transcendentals=0),
        name="finish",
    )(parts, coords)
    stress = pl.pallas_call(
        stress_kernel,
        out_shape=jax.ShapeDtypeStruct((1, 1), F32),
        name="stress",
    )(shares)
    return (new_coords, stress[0, 0])


def solution(mesh):
    n_row, n_col, n_depth = (mesh.shape[a] for a in ("row", "col", "depth"))
    fine = jax.sharding.Mesh(
        mesh.devices.reshape(n_row, n_col // 2, 2, n_depth), ("row", "z", "core", "depth")
    )
    points = P(None, ("row", "z", "core", "depth"))
    return jax.shard_map(
        shards,
        mesh=fine,
        in_specs=(points, points, P("row", ("z", "core", "depth"))),
        out_specs=(points, P()),
        check_vma=False,
    )
```

```python
import jax
import jax.numpy as jnp
from jax import lax
from jax.experimental import pallas as pl
from jax.experimental.pallas import tpu as pltpu
from jax.sharding import PartitionSpec as P

F32 = jnp.float32
BF16 = jnp.bfloat16

EMB, XH, XL, XH2, QF, QX, ONE, LANES = 0, 64, 80, 96, 112, 115, 118, 128
TINY = 1e-30


def bilinear_form(kind):
    a = lax.broadcasted_iota(jnp.int32, (LANES, LANES), 0)
    b = lax.broadcasted_iota(jnp.int32, (LANES, LANES), 1)

    def band(first, count, shift):
        return (a >= first) & (a < first + count) & (b == a + shift)

    if kind == 0:
        cross = band(EMB, 64, 0)
        square, unit = QF, 1.0 / 64.0
    else:
        cross = band(XH, 16, 0) | band(XL, 16, XH2 - XL) | band(XH2, 16, XL - XH2)
        square, unit = QX, 1.0
    norms = band(square, 3, ONE - square) | band(ONE, 3, square - ONE)
    return jnp.where(cross, -2.0 * unit, jnp.where(norms, unit, 0.0)).astype(BF16)


def split3(value):
    hi = value.astype(BF16).astype(F32)
    mid = (value - hi).astype(BF16).astype(F32)
    low = (value - hi - mid).astype(BF16).astype(F32)
    return hi, mid, low


def pack_kernel(emb_ref, crd_ref, own_ref, out_ref):
    emb = emb_ref[...].astype(F32)
    crd = crd_ref[...]
    hi = crd.astype(BF16).astype(F32)
    feats = jnp.concatenate([emb, hi, crd - hi], axis=0)
    half = feats.shape[0] // 2
    mine = jnp.concatenate([feats[:half], feats[half:]], axis=1).astype(BF16)
    own_ref[...] = mine
    for k in range(out_ref.shape[0]):
        out_ref[k] = mine


def unpack(shards):
    top, low = [], []
    for sh in shards:
        sh = sh.astype(F32)
        top.append(sh[:, 0:64])
        low.append(sh[:, 64:128])
    feats = jnp.concatenate([jnp.concatenate(top, axis=1), jnp.concatenate(low, axis=1)], axis=0)
    emb, hi, low = feats[0:64], feats[XH : XH + 16], feats[XL : XL + 16]
    crd = hi + low
    squares = split3(jnp.sum(emb * emb, axis=0, keepdims=True))
    squares += split3(jnp.sum(crd * crd, axis=0, keepdims=True))
    at = lax.broadcasted_iota(jnp.int32, (16, feats.shape[1]), 0)
    tail = jnp.where((at >= ONE - QF) & (at < ONE - QF + 3), 1.0, 0.0)
    for k, sq in enumerate(squares):
        tail = jnp.where(at == k, sq, tail)
    return jnp.concatenate([feats, hi, tail], axis=0)


def spread_kernel(own_ref, out_ref):
    own = own_ref[...]
    for k in range(out_ref.shape[0]):
        out_ref[k] = own


def pairs_kernel(own_ref, oth_ref, col_ref, w_hbm, out_ref, w_ref, f_scr, x_scr, flat_scr, rows_scr, c_scr, f_tiles, x_tiles, sems):
    total_rows, total = w_ref.shape
    tm = c_scr.shape[0]
    tn = min(256, total)
    steps = total_rows // tm
    first = lax.axis_index("core") == 0

    def fetch(i):
        at = pl.ds(i * tm, tm)
        return pltpu.make_async_copy(w_hbm.at[at, :], w_ref.at[at, :], sems.at[i])

    for i in range(steps):
        fetch(i).start()
    last = (((1,), (1,)), ((), ()))
    form_f = bilinear_form(0)
    form_x = bilinear_form(1)
    for s in range(0, col_ref.shape[0], 4):
        some = unpack([col_ref[k] for k in range(s, min(s + 4, col_ref.shape[0]))]).astype(BF16)
        cut = slice(64 * s, 64 * s + some.shape[1])
        flat_scr[:, cut] = some
        f_scr[:, cut] = jnp.dot(form_f, some, preferred_element_type=F32).astype(BF16)
        x_scr[:, cut] = jnp.dot(form_x, some, preferred_element_type=F32).astype(BF16)

    def row_block(i, slot):
        shards = []
        for k in range(tm // 256):
            at = i * (tm // 128) + 2 * k
            own = [own_ref[at], own_ref[at + 1]]
            oth = [oth_ref[at], oth_ref[at + 1]]
            shards += [jnp.where(first, a, b) for a, b in zip(own, oth)]
            shards += [jnp.where(first, b, a) for a, b in zip(own, oth)]
        feats = unpack(shards)
        rows_scr[slot] = feats.astype(BF16)
        return feats.T.astype(BF16)

    def squares(rows, slot, cut):
        f_tiles[slot, :, cut] = jnp.dot(rows, f_scr[:, cut], preferred_element_type=F32)
        x_tiles[slot, :, cut] = jnp.dot(rows, x_scr[:, cut], preferred_element_type=F32)

    def chain(base, slot, cut, mis):
        for r in range(0, tm, 32):
            f2 = jnp.maximum(f_tiles[slot, r : r + 32, cut], TINY)
            x2 = jnp.maximum(x_tiles[slot, r : r + 32, cut], TINY)
            w = w_ref[pl.ds(pl.multiple_of(base + r, 32), 32), cut].astype(F32)
            dissim = f2 * lax.rsqrt(f2)
            inv = lax.rsqrt(x2)
            diff = dissim - x2 * inv
            c_scr[r : r + 32, cut] = (w * (dissim * jnp.minimum(inv, 1.0))).astype(BF16)
            miss = w * (diff * diff)
            mis += (miss[0:8] + miss[8:16]) + (miss[16:24] + miss[24:32])
        return mis

    tiles = [slice(start, start + tn) for start in range(0, total, tn)]

    def block(i, slot, mis, scl, more=True):
        fetch(i).wait()
        if more:
            rows = row_block(i + 1, 1 - slot)
        bent = jnp.dot(form_f, rows_scr[slot], preferred_element_type=F32)
        base = i * tm
        acc = jnp.zeros((48, tm), F32)
        wacc = jnp.zeros((LANES, tm), F32)
        for n in range(len(tiles) + 1):
            if n < len(tiles):
                cut = tiles[n]
                if more:
                    squares(rows, 1 - slot, cut)
                wb = w_ref[pl.ds(pl.multiple_of(base, tm), tm), cut]
                wacc += lax.dot_general(flat_scr[:, cut], wb, last, preferred_element_type=F32)
            if n > 0:
                old = tiles[n - 1]
                picked = jnp.concatenate([flat_scr[XH : XH + 32, old], flat_scr[QF:, old]], axis=0)
                acc += lax.dot_general(picked, c_scr[:, old], last, preferred_element_type=F32)
            if n < len(tiles):
                mis = chain(base, slot, cut, mis)
        scl += jnp.sum((bent * wacc).reshape(LANES // 8, 8, tm), axis=0)
        less = acc[0:32] - wacc[XH : XH + 32]
        pull = less[0:16] + less[16:32]
        wsum = wacc[ONE : ONE + 1]
        rate = acc[32 + ONE - QF : 33 + ONE - QF] - wsum
        for k in range(tm // 64):
            cut = slice(64 * k, 64 * k + 64)
            to = i * (tm // 64) + k
            for j in range(8):
                line = jnp.concatenate([pull[j : j + 1, cut], pull[j + 8 : j + 9, cut]], axis=1)
                out_ref[to, :, 128 * j : 128 * j + 128] = line
            out_ref[to, :, 1024:1152] = jnp.concatenate([rate[:, cut], wsum[:, cut]], axis=1)
        return mis, scl

    def two(k, carry):
        carry = block(2 * k, 0, *carry)
        return block(2 * k + 1, 1, *carry)

    squares(row_block(0, 0), 0, slice(0, total))
    pairs = (steps - 1) // 2
    sums = lax.fori_loop(0, pairs, two, (jnp.zeros((8, tn), F32), jnp.zeros((8, tm), F32)))
    for i in range(2 * pairs, steps):
        sums = block(i, i % 2, *sums, more=i + 1 < steps)
    mis, scl = sums
    mis = jnp.sum(jnp.sum(mis, axis=0, keepdims=True), axis=1, keepdims=True)
    scl = jnp.sum(jnp.sum(scl, axis=0, keepdims=True), axis=1, keepdims=True)
    at = lax.broadcasted_iota(jnp.int32, (1, 128), 1)
    line = jnp.where(at == 0, mis, jnp.where(at == 1, scl, 0.0))
    out_ref[:, :, 1152:1280] = jnp.broadcast_to(line[None], (out_ref.shape[0], 1, 128))


def finish_kernel(part_ref, crd_ref, new_ref):
    sums = jnp.sum(part_ref[...], axis=0)
    lines = [sums[:, 128 * k : 128 * k + 128] for k in range(9)]
    half = jnp.concatenate(lines[:8], axis=0)
    pull = jnp.concatenate([half[:, 0:64], half[:, 64:128]], axis=0)
    rate = lines[8][:, 0:64]
    wsum = lines[8][:, 64:128]
    crd = crd_ref[...]
    new_ref[...] = crd + (rate * crd - pull) / wsum


def stress_kernel(part_ref, out_ref):
    sums = jnp.sum(part_ref[...], axis=0)
    out_ref[...] = sums[:, 0:1] / sums[:, 1:2]


def column_moves(n_row, n_col, n_depth):
    moves = []
    for row in range(n_row):
        for at in range(n_col * n_depth):
            moves.append((row * n_col * n_depth + at, (at % n_row * n_col + row) * n_depth + at // n_row))
    return moves


def shards(embeddings, coords, pair_weight):
    rows, cols = pair_weight.shape
    points = embeddings.shape[1]
    group = rows // points
    n_row, n_z, n_core, n_depth = (lax.axis_size(a) for a in ("row", "z", "core", "depth"))
    likes = n_z * n_depth

    shard = (48, 128)
    packed = pl.pallas_call(
        pack_kernel,
        out_shape=(
            jax.ShapeDtypeStruct(shard, BF16),
            jax.ShapeDtypeStruct((likes,) + shard, BF16),
        ),
        name="pack",
    )(embeddings, coords)
    moves = column_moves(n_row, n_z * n_core, n_depth)
    moved = lax.ppermute(packed[0], ("row", "z", "core", "depth"), moves)
    own = lax.all_to_all(packed[1], ("z", "depth"), 0, 0, tiled=True)
    moved = pl.pallas_call(
        spread_kernel,
        out_shape=jax.ShapeDtypeStruct((n_row,) + shard, BF16),
        cost_estimate=pl.CostEstimate(flops=10**10, bytes_accessed=10**8, transcendentals=0),
        name="spread",
    )(moved)
    moved, own = lax.optimization_barrier((moved, own))
    oth = lax.ppermute(own, "core", [(0, 1), (1, 0)])
    t_cols = lax.all_to_all(moved, "row", 0, 0, tiled=True)

    vmem = pl.BlockSpec(memory_space=pltpu.VMEM)
    tm = 256
    parts = pl.pallas_call(
        pairs_kernel,
        in_specs=[
            vmem,
            vmem,
            vmem,
            pl.BlockSpec(memory_space=pltpu.HBM),
        ],
        out_specs=vmem,
        out_shape=jax.ShapeDtypeStruct((group, 1, 1280), F32),
        scratch_shapes=[
            pltpu.VMEM((rows, cols), BF16),
            pltpu.VMEM((LANES, cols), BF16),
            pltpu.VMEM((LANES, cols), BF16),
            pltpu.VMEM((LANES, cols), BF16),
            pltpu.VMEM((2, LANES, tm), BF16),
            pltpu.VMEM((tm, cols), BF16),
            pltpu.VMEM((2, tm, cols), F32),
            pltpu.VMEM((2, tm, cols), F32),
            pltpu.SemaphoreType.DMA((rows // tm,)),
        ],
        compiler_params=pltpu.CompilerParams(vmem_limit_bytes=52 * 1024 * 1024),
        name="pairs",
    )(own, oth, t_cols, pair_weight)
    parts = lax.all_to_all(parts, ("z", "core", "depth"), 0, 0, tiled=True)
    shares = jnp.sum(parts[:, :, 1152:], axis=0, keepdims=True)
    shares = lax.all_to_all(jnp.broadcast_to(shares, (n_row, 1, 128)), "row", 0, 0, tiled=True)
    new_coords = pl.pallas_call(
        finish_kernel,
        out_shape=jax.ShapeDtypeStruct(coords.shape, F32),
        cost_estimate=pl.CostEstimate(flops=100000, bytes_accessed=200000, transcendentals=0),
        name="finish",
    )(parts, coords)
    stress = pl.pallas_call(
        stress_kernel,
        out_shape=jax.ShapeDtypeStruct((1, 1), F32),
        name="stress",
    )(shares)
    return (new_coords, stress[0, 0])


def solution(mesh):
    n_row, n_col, n_depth = (mesh.shape[a] for a in ("row", "col", "depth"))
    fine = jax.sharding.Mesh(
        mesh.devices.reshape(n_row, n_col // 2, 2, n_depth), ("row", "z", "core", "depth")
    )
    points = P(None, ("row", "z", "core", "depth"))
    return jax.shard_map(
        shards,
        mesh=fine,
        in_specs=(points, points, P("row", ("z", "core", "depth"))),
        out_specs=(points, P()),
        check_vma=False,
    )
```

```python
import jax
import jax.numpy as jnp
from jax import lax
from jax.experimental import pallas as pl
from jax.experimental.pallas import tpu as pltpu
from jax.sharding import PartitionSpec as P

F32 = jnp.float32
BF16 = jnp.bfloat16

EMB, XH, XL, XH2, QF, QX, ONE, LANES = 0, 64, 80, 96, 112, 115, 118, 128
TINY = 1e-30


def bilinear_form(kind):
    a = lax.broadcasted_iota(jnp.int32, (LANES, LANES), 0)
    b = lax.broadcasted_iota(jnp.int32, (LANES, LANES), 1)

    def band(first, count, shift):
        return (a >= first) & (a < first + count) & (b == a + shift)

    if kind == 0:
        cross = band(EMB, 64, 0)
        square, unit = QF, 1.0 / 64.0
    else:
        cross = band(XH, 16, 0) | band(XL, 16, XH2 - XL) | band(XH2, 16, XL - XH2)
        square, unit = QX, 1.0
    norms = band(square, 3, ONE - square) | band(ONE, 3, square - ONE)
    return jnp.where(cross, -2.0 * unit, jnp.where(norms, unit, 0.0)).astype(BF16)


def split3(value):
    hi = value.astype(BF16).astype(F32)
    mid = (value - hi).astype(BF16).astype(F32)
    low = (value - hi - mid).astype(BF16).astype(F32)
    return hi, mid, low


def pack_kernel(emb_ref, crd_ref, own_ref, out_ref):
    emb = emb_ref[...].astype(F32)
    crd = crd_ref[...]
    hi = crd.astype(BF16).astype(F32)
    feats = jnp.concatenate([emb, hi, crd - hi], axis=0)
    half = feats.shape[0] // 2
    mine = jnp.concatenate([feats[:half], feats[half:]], axis=1).astype(BF16)
    own_ref[...] = mine
    for k in range(out_ref.shape[0]):
        out_ref[k] = mine


def unpack(shards):
    top, low = [], []
    for sh in shards:
        sh = sh.astype(F32)
        top.append(sh[:, 0:64])
        low.append(sh[:, 64:128])
    feats = jnp.concatenate([jnp.concatenate(top, axis=1), jnp.concatenate(low, axis=1)], axis=0)
    emb, hi, low = feats[0:64], feats[XH : XH + 16], feats[XL : XL + 16]
    crd = hi + low
    squares = split3(jnp.sum(emb * emb, axis=0, keepdims=True))
    squares += split3(jnp.sum(crd * crd, axis=0, keepdims=True))
    at = lax.broadcasted_iota(jnp.int32, (16, feats.shape[1]), 0)
    tail = jnp.where((at >= ONE - QF) & (at < ONE - QF + 3), 1.0, 0.0)
    for k, sq in enumerate(squares):
        tail = jnp.where(at == k, sq, tail)
    return jnp.concatenate([feats, hi, tail], axis=0)


def spread_kernel(own_ref, out_ref):
    own = own_ref[...]
    for k in range(out_ref.shape[0]):
        out_ref[k] = own


def pairs_kernel(own_ref, oth_ref, col_ref, w_hbm, out_ref, w_ref, f_scr, x_scr, flat_scr, rows_scr, c_scr, f_tiles, x_tiles, sems):
    total_rows, total = w_ref.shape
    tm = c_scr.shape[0]
    tn = min(256, total)
    steps = total_rows // tm
    first = lax.axis_index("core") == 0

    def fetch(i):
        at = pl.ds(i * tm, tm)
        return pltpu.make_async_copy(w_hbm.at[at, :], w_ref.at[at, :], sems.at[i])

    for i in range(steps):
        fetch(i).start()
    last = (((1,), (1,)), ((), ()))
    form_f = bilinear_form(0)
    form_x = bilinear_form(1)
    for s in range(0, col_ref.shape[0], 4):
        some = unpack([col_ref[k] for k in range(s, min(s + 4, col_ref.shape[0]))]).astype(BF16)
        cut = slice(64 * s, 64 * s + some.shape[1])
        flat_scr[:, cut] = some
        f_scr[:, cut] = jnp.dot(form_f, some, preferred_element_type=F32).astype(BF16)
        x_scr[:, cut] = jnp.dot(form_x, some, preferred_element_type=F32).astype(BF16)

    def row_block(i, slot):
        shards = []
        for k in range(tm // 256):
            at = i * (tm // 128) + 2 * k
            own = [own_ref[at], own_ref[at + 1]]
            oth = [oth_ref[at], oth_ref[at + 1]]
            shards += [jnp.where(first, a, b) for a, b in zip(own, oth)]
            shards += [jnp.where(first, b, a) for a, b in zip(own, oth)]
        feats = unpack(shards)
        rows_scr[slot] = feats.astype(BF16)
        return feats.T.astype(BF16)

    def squares(rows, slot, cut):
        f_tiles[slot, :, cut] = jnp.dot(rows, f_scr[:, cut], preferred_element_type=F32)
        x_tiles[slot, :, cut] = jnp.dot(rows, x_scr[:, cut], preferred_element_type=F32)

    def chain(base, slot, cut, mis):
        for r in range(0, tm, 32):
            f2 = jnp.maximum(f_tiles[slot, r : r + 32, cut], TINY)
            x2 = jnp.maximum(x_tiles[slot, r : r + 32, cut], TINY)
            w = w_ref[pl.ds(pl.multiple_of(base + r, 32), 32), cut].astype(F32)
            dissim = f2 * lax.rsqrt(f2)
            inv = lax.rsqrt(x2)
            diff = dissim - x2 * inv
            c_scr[r : r + 32, cut] = (w * (dissim * jnp.minimum(inv, 1.0))).astype(BF16)
            miss = w * (diff * diff)
            mis += (miss[0:8] + miss[8:16]) + (miss[16:24] + miss[24:32])
        return mis

    tiles = [slice(start, start + tn) for start in range(0, total, tn)]

    def block(i, slot, mis, scl, more=True):
        fetch(i).wait()
        if more:
            rows = row_block(i + 1, 1 - slot)
        bent = jnp.dot(form_f, rows_scr[slot], preferred_element_type=F32)
        base = i * tm
        acc = jnp.zeros((48, tm), F32)
        wacc = jnp.zeros((LANES, tm), F32)
        for n in range(len(tiles) + 1):
            if n < len(tiles):
                cut = tiles[n]
                if more:
                    squares(rows, 1 - slot, cut)
                wb = w_ref[pl.ds(pl.multiple_of(base, tm), tm), cut]
                wacc += lax.dot_general(flat_scr[:, cut], wb, last, preferred_element_type=F32)
            if n > 0:
                old = tiles[n - 1]
                picked = jnp.concatenate([flat_scr[XH : XH + 32, old], flat_scr[QF:, old]], axis=0)
                acc += lax.dot_general(picked, c_scr[:, old], last, preferred_element_type=F32)
            if n < len(tiles):
                mis = chain(base, slot, cut, mis)
        scl += jnp.sum((bent * wacc).reshape(LANES // 8, 8, tm), axis=0)
        less = acc[0:32] - wacc[XH : XH + 32]
        pull = less[0:16] + less[16:32]
        wsum = wacc[ONE : ONE + 1]
        rate = acc[32 + ONE - QF : 33 + ONE - QF] - wsum
        for k in range(tm // 64):
            cut = slice(64 * k, 64 * k + 64)
            to = i * (tm // 64) + k
            for j in range(8):
                line = jnp.concatenate([pull[j : j + 1, cut], pull[j + 8 : j + 9, cut]], axis=1)
                out_ref[to, :, 128 * j : 128 * j + 128] = line
            out_ref[to, :, 1024:1152] = jnp.concatenate([rate[:, cut], wsum[:, cut]], axis=1)
        return mis, scl

    def two(k, carry):
        carry = block(2 * k, 0, *carry)
        return block(2 * k + 1, 1, *carry)

    squares(row_block(0, 0), 0, slice(0, total))
    pairs = (steps - 1) // 2
    sums = lax.fori_loop(0, pairs, two, (jnp.zeros((8, tn), F32), jnp.zeros((8, tm), F32)))
    for i in range(2 * pairs, steps):
        sums = block(i, i % 2, *sums, more=i + 1 < steps)
    mis, scl = sums
    mis = jnp.sum(jnp.sum(mis, axis=0, keepdims=True), axis=1, keepdims=True)
    scl = jnp.sum(jnp.sum(scl, axis=0, keepdims=True), axis=1, keepdims=True)
    at = lax.broadcasted_iota(jnp.int32, (1, 128), 1)
    line = jnp.where(at == 0, mis, jnp.where(at == 1, scl, 0.0))
    out_ref[:, :, 1152:1280] = jnp.broadcast_to(line[None], (out_ref.shape[0], 1, 128))


def finish_kernel(part_ref, crd_ref, new_ref):
    sums = jnp.sum(part_ref[...], axis=0)
    lines = [sums[:, 128 * k : 128 * k + 128] for k in range(9)]
    half = jnp.concatenate(lines[:8], axis=0)
    pull = jnp.concatenate([half[:, 0:64], half[:, 64:128]], axis=0)
    rate = lines[8][:, 0:64]
    wsum = lines[8][:, 64:128]
    crd = crd_ref[...]
    new_ref[...] = crd + (rate * crd - pull) / wsum


def stress_kernel(part_ref, out_ref):
    sums = jnp.sum(part_ref[...], axis=0)
    out_ref[...] = sums[:, 0:1] / sums[:, 1:2]


def column_moves(n_row, n_col, n_depth):
    moves = []
    for row in range(n_row):
        for at in range(n_col * n_depth):
            moves.append((row * n_col * n_depth + at, (at % n_row * n_col + row) * n_depth + at // n_row))
    return moves


def shards(embeddings, coords, pair_weight):
    rows, cols = pair_weight.shape
    points = embeddings.shape[1]
    group = rows // points
    n_row, n_z, n_core, n_depth = (lax.axis_size(a) for a in ("row", "z", "core", "depth"))
    likes = n_z * n_depth

    shard = (48, 128)
    packed = pl.pallas_call(
        pack_kernel,
        out_shape=(
            jax.ShapeDtypeStruct(shard, BF16),
            jax.ShapeDtypeStruct((likes,) + shard, BF16),
        ),
        name="pack",
    )(embeddings, coords)
    moves = column_moves(n_row, n_z * n_core, n_depth)
    moved = lax.ppermute(packed[0], ("row", "z", "core", "depth"), moves)
    own = lax.all_to_all(packed[1], ("z", "depth"), 0, 0, tiled=True)
    moved = pl.pallas_call(
        spread_kernel,
        out_shape=jax.ShapeDtypeStruct((n_row,) + shard, BF16),
        cost_estimate=pl.CostEstimate(flops=10**10, bytes_accessed=10**8, transcendentals=0),
        name="spread",
    )(moved)
    moved, own = lax.optimization_barrier((moved, own))
    oth = lax.ppermute(own, "core", [(0, 1), (1, 0)])
    t_cols = lax.all_to_all(moved, "row", 0, 0, tiled=True)

    vmem = pl.BlockSpec(memory_space=pltpu.VMEM)
    tm = min(512, rows)
    parts = pl.pallas_call(
        pairs_kernel,
        in_specs=[
            vmem,
            vmem,
            vmem,
            pl.BlockSpec(memory_space=pltpu.HBM),
        ],
        out_specs=vmem,
        out_shape=jax.ShapeDtypeStruct((group, 1, 1280), F32),
        scratch_shapes=[
            pltpu.VMEM((rows, cols), BF16),
            pltpu.VMEM((LANES, cols), BF16),
            pltpu.VMEM((LANES, cols), BF16),
            pltpu.VMEM((LANES, cols), BF16),
            pltpu.VMEM((2, LANES, tm), BF16),
            pltpu.VMEM((tm, cols), BF16),
            pltpu.VMEM((2, tm, cols), F32),
            pltpu.VMEM((2, tm, cols), F32),
            pltpu.SemaphoreType.DMA((rows // tm,)),
        ],
        compiler_params=pltpu.CompilerParams(vmem_limit_bytes=52 * 1024 * 1024),
        name="pairs",
    )(own, oth, t_cols, pair_weight)
    parts = lax.all_to_all(parts, ("z", "core", "depth"), 0, 0, tiled=True)
    shares = jnp.sum(parts[:, :, 1152:], axis=0, keepdims=True)
    shares = lax.all_to_all(jnp.broadcast_to(shares, (n_row, 1, 128)), "row", 0, 0, tiled=True)
    new_coords = pl.pallas_call(
        finish_kernel,
        out_shape=jax.ShapeDtypeStruct(coords.shape, F32),
        cost_estimate=pl.CostEstimate(flops=100000, bytes_accessed=200000, transcendentals=0),
        name="finish",
    )(parts, coords)
    stress = pl.pallas_call(
        stress_kernel,
        out_shape=jax.ShapeDtypeStruct((1, 1), F32),
        name="stress",
    )(shares)
    return (new_coords, stress[0, 0])


def solution(mesh):
    n_row, n_col, n_depth = (mesh.shape[a] for a in ("row", "col", "depth"))
    fine = jax.sharding.Mesh(
        mesh.devices.reshape(n_row, n_col // 2, 2, n_depth), ("row", "z", "core", "depth")
    )
    points = P(None, ("row", "z", "core", "depth"))
    return jax.shard_map(
        shards,
        mesh=fine,
        in_specs=(points, points, P("row", ("z", "core", "depth"))),
        out_specs=(points, P()),
        check_vma=False,
    )
```

```python
import jax
import jax.numpy as jnp
from jax import lax
from jax.experimental import pallas as pl
from jax.experimental.pallas import tpu as pltpu
from jax.sharding import PartitionSpec as P

F32 = jnp.float32
BF16 = jnp.bfloat16

EMB, XH, XL, XH2, QF, QX, ONE, LANES = 0, 64, 80, 96, 112, 115, 118, 128
TINY = 1e-30


def bilinear_form(kind):
    a = lax.broadcasted_iota(jnp.int32, (LANES, LANES), 0)
    b = lax.broadcasted_iota(jnp.int32, (LANES, LANES), 1)

    def band(first, count, shift):
        return (a >= first) & (a < first + count) & (b == a + shift)

    if kind == 0:
        cross = band(EMB, 64, 0)
        square, unit = QF, 1.0 / 64.0
    else:
        cross = band(XH, 16, 0) | band(XL, 16, XH2 - XL) | band(XH2, 16, XL - XH2)
        square, unit = QX, 1.0
    norms = band(square, 3, ONE - square) | band(ONE, 3, square - ONE)
    return jnp.where(cross, -2.0 * unit, jnp.where(norms, unit, 0.0)).astype(BF16)


def split3(value):
    hi = value.astype(BF16).astype(F32)
    mid = (value - hi).astype(BF16).astype(F32)
    low = (value - hi - mid).astype(BF16).astype(F32)
    return hi, mid, low


def pack_kernel(emb_ref, crd_ref, own_ref, out_ref):
    emb = emb_ref[...].astype(F32)
    crd = crd_ref[...]
    hi = crd.astype(BF16).astype(F32)
    feats = jnp.concatenate([emb, hi, crd - hi], axis=0)
    half = feats.shape[0] // 2
    mine = jnp.concatenate([feats[:half], feats[half:]], axis=1).astype(BF16)
    own_ref[...] = mine
    for k in range(out_ref.shape[0]):
        out_ref[k] = mine


def unpack(shards):
    top, low = [], []
    for sh in shards:
        sh = sh.astype(F32)
        top.append(sh[:, 0:64])
        low.append(sh[:, 64:128])
    feats = jnp.concatenate([jnp.concatenate(top, axis=1), jnp.concatenate(low, axis=1)], axis=0)
    emb, hi, low = feats[0:64], feats[XH : XH + 16], feats[XL : XL + 16]
    crd = hi + low
    squares = split3(jnp.sum(emb * emb, axis=0, keepdims=True))
    squares += split3(jnp.sum(crd * crd, axis=0, keepdims=True))
    at = lax.broadcasted_iota(jnp.int32, (16, feats.shape[1]), 0)
    tail = jnp.where((at >= ONE - QF) & (at < ONE - QF + 3), 1.0, 0.0)
    for k, sq in enumerate(squares):
        tail = jnp.where(at == k, sq, tail)
    return jnp.concatenate([feats, hi, tail], axis=0)


def spread_kernel(own_ref, out_ref):
    own = own_ref[...]
    for k in range(out_ref.shape[0]):
        out_ref[k] = own


def rows_kernel(own_ref, oth_ref, out_ref):
    first = lax.axis_index("core") == 0
    for z in range(own_ref.shape[0] // 2):
        own = [own_ref[2 * z], own_ref[2 * z + 1]]
        oth = [oth_ref[2 * z], oth_ref[2 * z + 1]]
        shards = [jnp.where(first, a, b) for a, b in zip(own, oth)]
        shards += [jnp.where(first, b, a) for a, b in zip(own, oth)]
        out_ref[256 * z : 256 * z + 256, :] = unpack(shards).T.astype(BF16)


def pairs_kernel(row_ref, col_ref, w_hbm, out_ref, w_ref, f_scr, x_scr, flat_scr, c_scr, f_tiles, x_tiles, sems):
    total_rows, total = w_ref.shape
    tm = c_scr.shape[0]
    tn = min(256, total)
    steps = total_rows // tm

    def fetch(i):
        at = pl.ds(i * tm, tm)
        return pltpu.make_async_copy(w_hbm.at[at, :], w_ref.at[at, :], sems.at[i])

    for i in range(steps):
        fetch(i).start()
    last = (((1,), (1,)), ((), ()))
    form_f = bilinear_form(0)
    form_x = bilinear_form(1)
    for s in range(0, col_ref.shape[0], 4):
        some = unpack([col_ref[k] for k in range(s, min(s + 4, col_ref.shape[0]))]).astype(BF16)
        cut = slice(64 * s, 64 * s + some.shape[1])
        flat_scr[:, cut] = some
        f_scr[:, cut] = jnp.dot(form_f, some, preferred_element_type=F32).astype(BF16)
        x_scr[:, cut] = jnp.dot(form_x, some, preferred_element_type=F32).astype(BF16)

    def row_block(i):
        return row_ref[pl.ds(pl.multiple_of(i * tm, tm), tm), :]

    def squares(rows, slot, cut):
        f_tiles[slot, :, cut] = jnp.dot(rows, f_scr[:, cut], preferred_element_type=F32)
        x_tiles[slot, :, cut] = jnp.dot(rows, x_scr[:, cut], preferred_element_type=F32)

    def chain(base, slot, cut, mis):
        for r in range(0, tm, 32):
            f2 = jnp.maximum(f_tiles[slot, r : r + 32, cut], TINY)
            x2 = jnp.maximum(x_tiles[slot, r : r + 32, cut], TINY)
            w = w_ref[pl.ds(pl.multiple_of(base + r, 32), 32), cut].astype(F32)
            dissim = f2 * lax.rsqrt(f2)
            inv = lax.rsqrt(x2)
            diff = dissim - x2 * inv
            c_scr[r : r + 32, cut] = (w * (dissim * jnp.minimum(inv, 1.0))).astype(BF16)
            miss = w * (diff * diff)
            mis += (miss[0:8] + miss[8:16]) + (miss[16:24] + miss[24:32])
        return mis

    tiles = [slice(start, start + tn) for start in range(0, total, tn)]

    def block(i, slot, mis, scl, more=True):
        fetch(i).wait()
        if more:
            rows = row_block(i + 1)
        bent = lax.dot_general(form_f, row_block(i), last, preferred_element_type=F32)
        base = i * tm
        acc = jnp.zeros((48, tm), F32)
        wacc = jnp.zeros((LANES, tm), F32)
        for n in range(len(tiles) + 1):
            if n < len(tiles):
                cut = tiles[n]
                if more:
                    squares(rows, 1 - slot, cut)
                wb = w_ref[pl.ds(pl.multiple_of(base, tm), tm), cut]
                wacc += lax.dot_general(flat_scr[:, cut], wb, last, preferred_element_type=F32)
            if n > 0:
                old = tiles[n - 1]
                picked = jnp.concatenate([flat_scr[XH : XH + 32, old], flat_scr[QF:, old]], axis=0)
                acc += lax.dot_general(picked, c_scr[:, old], last, preferred_element_type=F32)
            if n < len(tiles):
                mis = chain(base, slot, cut, mis)
        scl += jnp.sum((bent * wacc).reshape(LANES // 8, 8, tm), axis=0)
        less = acc[0:32] - wacc[XH : XH + 32]
        pull = less[0:16] + less[16:32]
        wsum = wacc[ONE : ONE + 1]
        rate = acc[32 + ONE - QF : 33 + ONE - QF] - wsum
        for k in range(tm // 64):
            cut = slice(64 * k, 64 * k + 64)
            to = i * (tm // 64) + k
            for j in range(8):
                line = jnp.concatenate([pull[j : j + 1, cut], pull[j + 8 : j + 9, cut]], axis=1)
                out_ref[to, :, 128 * j : 128 * j + 128] = line
            out_ref[to, :, 1024:1152] = jnp.concatenate([rate[:, cut], wsum[:, cut]], axis=1)
        return mis, scl

    def two(k, carry):
        carry = block(2 * k, 0, *carry)
        return block(2 * k + 1, 1, *carry)

    squares(row_block(0), 0, slice(0, total))
    pairs = (steps - 1) // 2
    sums = lax.fori_loop(0, pairs, two, (jnp.zeros((8, tn), F32), jnp.zeros((8, tm), F32)))
    for i in range(2 * pairs, steps):
        sums = block(i, i % 2, *sums, more=i + 1 < steps)
    mis, scl = sums
    mis = jnp.sum(jnp.sum(mis, axis=0, keepdims=True), axis=1, keepdims=True)
    scl = jnp.sum(jnp.sum(scl, axis=0, keepdims=True), axis=1, keepdims=True)
    at = lax.broadcasted_iota(jnp.int32, (1, 128), 1)
    line = jnp.where(at == 0, mis, jnp.where(at == 1, scl, 0.0))
    out_ref[:, :, 1152:1280] = jnp.broadcast_to(line[None], (out_ref.shape[0], 1, 128))


def finish_kernel(part_ref, crd_ref, new_ref):
    sums = jnp.sum(part_ref[...], axis=0)
    lines = [sums[:, 128 * k : 128 * k + 128] for k in range(9)]
    half = jnp.concatenate(lines[:8], axis=0)
    pull = jnp.concatenate([half[:, 0:64], half[:, 64:128]], axis=0)
    rate = lines[8][:, 0:64]
    wsum = lines[8][:, 64:128]
    crd = crd_ref[...]
    new_ref[...] = crd + (rate * crd - pull) / wsum


def stress_kernel(part_ref, out_ref):
    sums = jnp.sum(part_ref[...], axis=0)
    out_ref[...] = sums[:, 0:1] / sums[:, 1:2]


def column_moves(n_row, n_col, n_depth):
    moves = []
    for row in range(n_row):
        for at in range(n_col * n_depth):
            moves.append((row * n_col * n_depth + at, (at % n_row * n_col + row) * n_depth + at // n_row))
    return moves


def shards(embeddings, coords, pair_weight):
    rows, cols = pair_weight.shape
    points = embeddings.shape[1]
    group = rows // points
    n_row, n_z, n_core, n_depth = (lax.axis_size(a) for a in ("row", "z", "core", "depth"))
    likes = n_z * n_depth

    shard = (48, 128)
    packed = pl.pallas_call(
        pack_kernel,
        out_shape=(
            jax.ShapeDtypeStruct(shard, BF16),
            jax.ShapeDtypeStruct((likes,) + shard, BF16),
        ),
        name="pack",
    )(embeddings, coords)
    moves = column_moves(n_row, n_z * n_core, n_depth)
    moved = lax.ppermute(packed[0], ("row", "z", "core", "depth"), moves)
    own = lax.all_to_all(packed[1], ("z", "depth"), 0, 0, tiled=True)
    moved = pl.pallas_call(
        spread_kernel,
        out_shape=jax.ShapeDtypeStruct((n_row,) + shard, BF16),
        cost_estimate=pl.CostEstimate(flops=10**10, bytes_accessed=10**8, transcendentals=0),
        name="spread",
    )(moved)
    moved, own = lax.optimization_barrier((moved, own))
    oth = lax.ppermute(own, "core", [(0, 1), (1, 0)])
    t_cols = lax.all_to_all(moved, "row", 0, 0, tiled=True)
    t_rows = pl.pallas_call(
        rows_kernel,
        out_shape=jax.ShapeDtypeStruct((rows, LANES), BF16),
        cost_estimate=pl.CostEstimate(flops=10**10, bytes_accessed=10**8, transcendentals=0),
        name="rows",
    )(own, oth)

    vmem = pl.BlockSpec(memory_space=pltpu.VMEM)
    tm = 256
    parts = pl.pallas_call(
        pairs_kernel,
        in_specs=[
            vmem,
            vmem,
            pl.BlockSpec(memory_space=pltpu.HBM),
        ],
        out_specs=vmem,
        out_shape=jax.ShapeDtypeStruct((group, 1, 1280), F32),
        scratch_shapes=[
            pltpu.VMEM((rows, cols), BF16),
            pltpu.VMEM((LANES, cols), BF16),
            pltpu.VMEM((LANES, cols), BF16),
            pltpu.VMEM((LANES, cols), BF16),
            pltpu.VMEM((tm, cols), BF16),
            pltpu.VMEM((2, tm, cols), F32),
            pltpu.VMEM((2, tm, cols), F32),
            pltpu.SemaphoreType.DMA((rows // tm,)),
        ],
        compiler_params=pltpu.CompilerParams(vmem_limit_bytes=52 * 1024 * 1024),
        name="pairs",
    )(t_rows, t_cols, pair_weight)
    parts = lax.all_to_all(parts, ("z", "core", "depth"), 0, 0, tiled=True)
    shares = jnp.sum(parts[:, :, 1152:], axis=0, keepdims=True)
    shares = lax.all_to_all(jnp.broadcast_to(shares, (n_row, 1, 128)), "row", 0, 0, tiled=True)
    new_coords = pl.pallas_call(
        finish_kernel,
        out_shape=jax.ShapeDtypeStruct(coords.shape, F32),
        cost_estimate=pl.CostEstimate(flops=100000, bytes_accessed=200000, transcendentals=0),
        name="finish",
    )(parts, coords)
    stress = pl.pallas_call(
        stress_kernel,
        out_shape=jax.ShapeDtypeStruct((1, 1), F32),
        name="stress",
    )(shares)
    return (new_coords, stress[0, 0])


def solution(mesh):
    n_row, n_col, n_depth = (mesh.shape[a] for a in ("row", "col", "depth"))
    fine = jax.sharding.Mesh(
        mesh.devices.reshape(n_row, n_col // 2, 2, n_depth), ("row", "z", "core", "depth")
    )
    points = P(None, ("row", "z", "core", "depth"))
    return jax.shard_map(
        shards,
        mesh=fine,
        in_specs=(points, points, P("row", ("z", "core", "depth"))),
        out_specs=(points, P()),
        check_vma=False,
    )
```

```python
import jax
import jax.numpy as jnp
from jax import lax
from jax.experimental import pallas as pl
from jax.experimental.pallas import tpu as pltpu
from jax.sharding import PartitionSpec as P

F32 = jnp.float32
BF16 = jnp.bfloat16

EMB, XH, XL, XH2, QF, QX, ONE, LANES = 0, 64, 80, 96, 112, 115, 118, 128
TINY = 1e-30


def bilinear_form(kind):
    a = lax.broadcasted_iota(jnp.int32, (LANES, LANES), 0)
    b = lax.broadcasted_iota(jnp.int32, (LANES, LANES), 1)

    def band(first, count, shift):
        return (a >= first) & (a < first + count) & (b == a + shift)

    if kind == 0:
        cross = band(EMB, 64, 0)
        square, unit = QF, 1.0 / 64.0
    else:
        cross = band(XH, 16, 0) | band(XL, 16, XH2 - XL) | band(XH2, 16, XL - XH2)
        square, unit = QX, 1.0
    norms = band(square, 3, ONE - square) | band(ONE, 3, square - ONE)
    return jnp.where(cross, -2.0 * unit, jnp.where(norms, unit, 0.0)).astype(BF16)


def split3(value):
    hi = value.astype(BF16).astype(F32)
    mid = (value - hi).astype(BF16).astype(F32)
    low = (value - hi - mid).astype(BF16).astype(F32)
    return hi, mid, low


def norm_rows(emb, crd):
    squares = split3(jnp.sum(emb * emb, axis=0, keepdims=True))
    squares += split3(jnp.sum(crd * crd, axis=0, keepdims=True))
    at = lax.broadcasted_iota(jnp.int32, (16, emb.shape[1]), 0)
    tail = jnp.where((at >= ONE - QF) & (at < ONE - QF + 3), 1.0, 0.0)
    for k, sq in enumerate(squares):
        tail = jnp.where(at == k, sq, tail)
    return tail


def pack_kernel(emb_ref, crd_ref, own_ref, out_ref):
    emb = emb_ref[...].astype(F32)
    crd = crd_ref[...]
    hi = crd.astype(BF16).astype(F32)
    low = (crd - hi).astype(BF16).astype(F32)
    feats = jnp.concatenate([emb, hi, low], axis=0)
    half = feats.shape[0] // 2
    own_ref[...] = jnp.concatenate([feats[:half], feats[half:]], axis=1).astype(BF16)
    mine = jnp.concatenate([feats, hi, norm_rows(emb, hi + low)], axis=0).T.astype(BF16)
    for k in range(out_ref.shape[0]):
        out_ref[k] = mine


def unpack(shards):
    top, low = [], []
    for sh in shards:
        sh = sh.astype(F32)
        top.append(sh[:, 0:64])
        low.append(sh[:, 64:128])
    feats = jnp.concatenate([jnp.concatenate(top, axis=1), jnp.concatenate(low, axis=1)], axis=0)
    hi, low = feats[XH : XH + 16], feats[XL : XL + 16]
    return jnp.concatenate([feats, hi, norm_rows(feats[0:64], hi + low)], axis=0)


def spread_kernel(own_ref, out_ref):
    own = own_ref[...]
    for k in range(out_ref.shape[0]):
        out_ref[k] = own


def pairs_kernel(own_ref, oth_ref, col_ref, w_hbm, out_ref, w_ref, f_scr, x_scr, flat_scr, c_scr, f_tiles, x_tiles, sems):
    total_rows, total = w_ref.shape
    tm = c_scr.shape[0]
    tn = min(256, total)
    steps = total_rows // tm
    first = lax.axis_index("core") == 0

    def fetch(i):
        at = pl.ds(i * tm, tm)
        return pltpu.make_async_copy(w_hbm.at[at, :], w_ref.at[at, :], sems.at[i])

    for i in range(steps):
        fetch(i).start()
    last = (((1,), (1,)), ((), ()))
    form_f = bilinear_form(0)
    form_x = bilinear_form(1)

    def row_block(i):
        pieces = []
        for k in range(tm // 256):
            cut = pl.ds(pl.multiple_of(i * (tm // 2) + k * 128, 128), 128)
            own, oth = own_ref[cut, :], oth_ref[cut, :]
            pieces += [jnp.where(first, own, oth), jnp.where(first, oth, own)]
        return jnp.concatenate(pieces, axis=0)

    def squares(rows, slot, cut):
        f_tiles[slot, :, cut] = jnp.dot(rows, f_scr[:, cut], preferred_element_type=F32)
        x_tiles[slot, :, cut] = jnp.dot(rows, x_scr[:, cut], preferred_element_type=F32)

    def chain(base, slot, cut, mis):
        for r in range(0, tm, 32):
            f2 = jnp.maximum(f_tiles[slot, r : r + 32, cut], TINY)
            x2 = jnp.maximum(x_tiles[slot, r : r + 32, cut], TINY)
            w = w_ref[pl.ds(pl.multiple_of(base + r, 32), 32), cut].astype(F32)
            dissim = f2 * lax.rsqrt(f2)
            inv = lax.rsqrt(x2)
            diff = dissim - x2 * inv
            c_scr[r : r + 32, cut] = (w * (dissim * jnp.minimum(inv, 1.0))).astype(BF16)
            miss = w * (diff * diff)
            mis += (miss[0:8] + miss[8:16]) + (miss[16:24] + miss[24:32])
        return mis

    tiles = [slice(start, start + tn) for start in range(0, total, tn)]

    def block(i, slot, mis, scl, more=True):
        fetch(i).wait()
        if more:
            rows = row_block(i + 1)
        bent = lax.dot_general(form_f, row_block(i), last, preferred_element_type=F32)
        base = i * tm
        acc = jnp.zeros((48, tm), F32)
        wacc = jnp.zeros((LANES, tm), F32)
        for n in range(len(tiles) + 1):
            if n < len(tiles):
                cut = tiles[n]
                if more:
                    squares(rows, 1 - slot, cut)
                wb = w_ref[pl.ds(pl.multiple_of(base, tm), tm), cut]
                wacc += lax.dot_general(flat_scr[:, cut], wb, last, preferred_element_type=F32)
            if n > 0:
                old = tiles[n - 1]
                picked = jnp.concatenate([flat_scr[XH : XH + 32, old], flat_scr[QF:, old]], axis=0)
                acc += lax.dot_general(picked, c_scr[:, old], last, preferred_element_type=F32)
            if n < len(tiles):
                mis = chain(base, slot, cut, mis)
        scl += jnp.sum((bent * wacc).reshape(LANES // 8, 8, tm), axis=0)
        less = acc[0:32] - wacc[XH : XH + 32]
        pull = less[0:16] + less[16:32]
        wsum = wacc[ONE : ONE + 1]
        rate = acc[32 + ONE - QF : 33 + ONE - QF] - wsum
        for k in range(tm // 64):
            cut = slice(64 * k, 64 * k + 64)
            to = i * (tm // 64) + k
            for j in range(8):
                line = jnp.concatenate([pull[j : j + 1, cut], pull[j + 8 : j + 9, cut]], axis=1)
                out_ref[to, :, 128 * j : 128 * j + 128] = line
            out_ref[to, :, 1024:1152] = jnp.concatenate([rate[:, cut], wsum[:, cut]], axis=1)
        return mis, scl

    def two(k, carry):
        carry = block(2 * k + 1, 1, *carry)
        return block(2 * k + 2, 0, *carry)

    rows = row_block(0)
    per = tn // 64
    for n, cut in enumerate(tiles):
        some = unpack([col_ref[k] for k in range(n * per, n * per + per)]).astype(BF16)
        flat_scr[:, cut] = some
        f_scr[:, cut] = jnp.dot(form_f, some, preferred_element_type=F32).astype(BF16)
        x_scr[:, cut] = jnp.dot(form_x, some, preferred_element_type=F32).astype(BF16)
        squares(rows, 0, cut)
    carry = (jnp.zeros((8, tn), F32), jnp.zeros((8, tm), F32))
    carry = block(0, 0, *carry, more=steps > 1)
    loops = max(0, (steps - 2) // 2)
    carry = lax.fori_loop(0, loops, two, carry)
    for i in range(2 * loops + 1, steps):
        carry = block(i, i % 2, *carry, more=i + 1 < steps)
    mis, scl = carry
    mis = jnp.sum(jnp.sum(mis, axis=0, keepdims=True), axis=1, keepdims=True)
    scl = jnp.sum(jnp.sum(scl, axis=0, keepdims=True), axis=1, keepdims=True)
    at = lax.broadcasted_iota(jnp.int32, (1, 128), 1)
    line = jnp.where(at == 0, mis, jnp.where(at == 1, scl, 0.0))
    out_ref[:, :, 1152:1280] = jnp.broadcast_to(line[None], (out_ref.shape[0], 1, 128))


def finish_kernel(part_ref, crd_ref, new_ref):
    sums = jnp.sum(part_ref[...], axis=0)
    lines = [sums[:, 128 * k : 128 * k + 128] for k in range(9)]
    half = jnp.concatenate(lines[:8], axis=0)
    pull = jnp.concatenate([half[:, 0:64], half[:, 64:128]], axis=0)
    rate = lines[8][:, 0:64]
    wsum = lines[8][:, 64:128]
    crd = crd_ref[...]
    new_ref[...] = crd + (rate * crd - pull) / wsum


def stress_kernel(part_ref, out_ref):
    sums = jnp.sum(part_ref[...], axis=0)
    out_ref[...] = sums[:, 0:1] / sums[:, 1:2]


def column_moves(n_row, n_col, n_depth):
    moves = []
    for row in range(n_row):
        for at in range(n_col * n_depth):
            moves.append((row * n_col * n_depth + at, (at % n_row * n_col + row) * n_depth + at // n_row))
    return moves


def shards(embeddings, coords, pair_weight):
    rows, cols = pair_weight.shape
    points = embeddings.shape[1]
    group = rows // points
    n_row, n_z, n_core, n_depth = (lax.axis_size(a) for a in ("row", "z", "core", "depth"))
    likes = n_z * n_depth

    shard = (48, 128)
    packed = pl.pallas_call(
        pack_kernel,
        out_shape=(
            jax.ShapeDtypeStruct(shard, BF16),
            jax.ShapeDtypeStruct((likes, points, LANES), BF16),
        ),
        name="pack",
    )(embeddings, coords)
    moves = column_moves(n_row, n_z * n_core, n_depth)
    moved = lax.ppermute(packed[0], ("row", "z", "core", "depth"), moves)
    own = lax.all_to_all(packed[1], ("z", "depth"), 0, 0, tiled=True)
    moved = pl.pallas_call(
        spread_kernel,
        out_shape=jax.ShapeDtypeStruct((n_row,) + shard, BF16),
        cost_estimate=pl.CostEstimate(flops=10**10, bytes_accessed=10**8, transcendentals=0),
        name="spread",
    )(moved)
    moved, own = lax.optimization_barrier((moved, own))
    own = own.reshape(rows // n_core, LANES)
    oth = lax.ppermute(own, "core", [(0, 1), (1, 0)])
    t_cols = lax.all_to_all(moved, "row", 0, 0, tiled=True)

    vmem = pl.BlockSpec(memory_space=pltpu.VMEM)
    tm = 256
    parts = pl.pallas_call(
        pairs_kernel,
        in_specs=[
            vmem,
            vmem,
            vmem,
            pl.BlockSpec(memory_space=pltpu.HBM),
        ],
        out_specs=vmem,
        out_shape=jax.ShapeDtypeStruct((group, 1, 1280), F32),
        scratch_shapes=[
            pltpu.VMEM((rows, cols), BF16),
            pltpu.VMEM((LANES, cols), BF16),
            pltpu.VMEM((LANES, cols), BF16),
            pltpu.VMEM((LANES, cols), BF16),
            pltpu.VMEM((tm, cols), BF16),
            pltpu.VMEM((2, tm, cols), F32),
            pltpu.VMEM((2, tm, cols), F32),
            pltpu.SemaphoreType.DMA((rows // tm,)),
        ],
        compiler_params=pltpu.CompilerParams(vmem_limit_bytes=52 * 1024 * 1024),
        name="pairs",
    )(own, oth, t_cols, pair_weight)
    parts = lax.all_to_all(parts, ("z", "core", "depth"), 0, 0, tiled=True)
    shares = jnp.sum(parts[:, :, 1152:], axis=0, keepdims=True)
    shares = lax.all_to_all(jnp.broadcast_to(shares, (n_row, 1, 128)), "row", 0, 0, tiled=True)
    new_coords = pl.pallas_call(
        finish_kernel,
        out_shape=jax.ShapeDtypeStruct(coords.shape, F32),
        cost_estimate=pl.CostEstimate(flops=100000, bytes_accessed=200000, transcendentals=0),
        name="finish",
    )(parts, coords)
    stress = pl.pallas_call(
        stress_kernel,
        out_shape=jax.ShapeDtypeStruct((1, 1), F32),
        name="stress",
    )(shares)
    return (new_coords, stress[0, 0])


def solution(mesh):
    n_row, n_col, n_depth = (mesh.shape[a] for a in ("row", "col", "depth"))
    fine = jax.sharding.Mesh(
        mesh.devices.reshape(n_row, n_col // 2, 2, n_depth), ("row", "z", "core", "depth")
    )
    points = P(None, ("row", "z", "core", "depth"))
    return jax.shard_map(
        shards,
        mesh=fine,
        in_specs=(points, points, P("row", ("z", "core", "depth"))),
        out_specs=(points, P()),
        check_vma=False,
    )
```

```python
import jax
import jax.numpy as jnp
from jax import lax
from jax.experimental import pallas as pl
from jax.experimental.pallas import tpu as pltpu
from jax.sharding import PartitionSpec as P

F32 = jnp.float32
BF16 = jnp.bfloat16

EMB, XH, XL, XH2, QF, QX, ONE, LANES = 0, 64, 80, 96, 112, 115, 118, 128
TINY = 1e-30


def bilinear_form(kind):
    a = lax.broadcasted_iota(jnp.int32, (LANES, LANES), 0)
    b = lax.broadcasted_iota(jnp.int32, (LANES, LANES), 1)

    def band(first, count, shift):
        return (a >= first) & (a < first + count) & (b == a + shift)

    if kind == 0:
        cross = band(EMB, 64, 0)
        square, unit = QF, 1.0 / 64.0
    else:
        cross = band(XH, 16, 0) | band(XL, 16, XH2 - XL) | band(XH2, 16, XL - XH2)
        square, unit = QX, 1.0
    norms = band(square, 3, ONE - square) | band(ONE, 3, square - ONE)
    return jnp.where(cross, -2.0 * unit, jnp.where(norms, unit, 0.0)).astype(BF16)


def split3(value):
    hi = value.astype(BF16).astype(F32)
    mid = (value - hi).astype(BF16).astype(F32)
    low = (value - hi - mid).astype(BF16).astype(F32)
    return hi, mid, low


def pack_kernel(emb_ref, crd_ref, own_ref, out_ref):
    emb = emb_ref[...].astype(F32)
    crd = crd_ref[...]
    hi = crd.astype(BF16).astype(F32)
    feats = jnp.concatenate([emb, hi, crd - hi], axis=0)
    half = feats.shape[0] // 2
    mine = jnp.concatenate([feats[:half], feats[half:]], axis=1).astype(BF16)
    own_ref[...] = mine
    for k in range(out_ref.shape[0]):
        out_ref[k] = mine


def unpack(shards):
    top, low = [], []
    for sh in shards:
        sh = sh.astype(F32)
        top.append(sh[:, 0:64])
        low.append(sh[:, 64:128])
    feats = jnp.concatenate([jnp.concatenate(top, axis=1), jnp.concatenate(low, axis=1)], axis=0)
    emb, hi, low = feats[0:64], feats[XH : XH + 16], feats[XL : XL + 16]
    crd = hi + low
    squares = split3(jnp.sum(emb * emb, axis=0, keepdims=True))
    squares += split3(jnp.sum(crd * crd, axis=0, keepdims=True))
    at = lax.broadcasted_iota(jnp.int32, (16, feats.shape[1]), 0)
    tail = jnp.where((at >= ONE - QF) & (at < ONE - QF + 3), 1.0, 0.0)
    for k, sq in enumerate(squares):
        tail = jnp.where(at == k, sq, tail)
    return jnp.concatenate([feats, hi, tail], axis=0)


def spread_kernel(own_ref, out_ref):
    own = own_ref[...]
    for k in range(out_ref.shape[0]):
        out_ref[k] = own


def pairs_kernel(own_ref, oth_ref, col_ref, w_hbm, out_ref, w_ref, f_scr, x_scr, flat_scr, rows_scr, feat_scr, c_scr, f_tiles, x_tiles, sems):
    total_rows, total = w_ref.shape
    tm = c_scr.shape[0]
    tn = min(256, total)
    steps = total_rows // tm
    first = lax.axis_index("core") == 0

    def fetch(i):
        at = pl.ds(i * tm, tm)
        return pltpu.make_async_copy(w_hbm.at[at, :], w_ref.at[at, :], sems.at[i])

    for i in range(steps):
        fetch(i).start()
    last = (((1,), (1,)), ((), ()))
    form_f = bilinear_form(0)
    form_x = bilinear_form(1)
    for s in range(0, col_ref.shape[0], 4):
        some = unpack([col_ref[k] for k in range(s, min(s + 4, col_ref.shape[0]))]).astype(BF16)
        cut = slice(64 * s, 64 * s + some.shape[1])
        flat_scr[:, cut] = some
        f_scr[:, cut] = jnp.dot(form_f, some, preferred_element_type=F32).astype(BF16)
        x_scr[:, cut] = jnp.dot(form_x, some, preferred_element_type=F32).astype(BF16)

    def row_block(i, slot):
        shards = []
        for k in range(tm // 256):
            at = i * (tm // 128) + 2 * k
            own = [own_ref[at], own_ref[at + 1]]
            oth = [oth_ref[at], oth_ref[at + 1]]
            shards += [jnp.where(first, a, b) for a, b in zip(own, oth)]
            shards += [jnp.where(first, b, a) for a, b in zip(own, oth)]
        feats = unpack(shards)
        feat_scr[slot] = feats.astype(BF16)
        rows_scr[slot] = feats.T.astype(BF16)

    def squares(slot, cut):
        rows = rows_scr[slot]
        f_tiles[slot, :, cut] = jnp.dot(rows, f_scr[:, cut], preferred_element_type=F32)
        x_tiles[slot, :, cut] = jnp.dot(rows, x_scr[:, cut], preferred_element_type=F32)

    def chain(base, slot, cut, mis):
        for r in range(0, tm, 32):
            f2 = jnp.maximum(f_tiles[slot, r : r + 32, cut], TINY)
            x2 = jnp.maximum(x_tiles[slot, r : r + 32, cut], TINY)
            w = w_ref[pl.ds(pl.multiple_of(base + r, 32), 32), cut].astype(F32)
            dissim = f2 * lax.rsqrt(f2)
            inv = lax.rsqrt(x2)
            diff = dissim - x2 * inv
            c_scr[r : r + 32, cut] = (w * (dissim * jnp.minimum(inv, 1.0))).astype(BF16)
            miss = w * (diff * diff)
            mis += (miss[0:8] + miss[8:16]) + (miss[16:24] + miss[24:32])
        return mis

    tiles = [slice(start, start + tn) for start in range(0, total, tn)]

    def block(i, slot, mis, scl, ahead=2):
        fetch(i).wait()
        bent = jnp.dot(form_f, feat_scr[slot], preferred_element_type=F32)
        base = i * tm
        acc = jnp.zeros((48, tm), F32)
        wacc = jnp.zeros((LANES, tm), F32)
        for n in range(len(tiles) + 1):
            if n < len(tiles):
                cut = tiles[n]
                if ahead > 0:
                    squares(1 - slot, cut)
                wb = w_ref[pl.ds(pl.multiple_of(base, tm), tm), cut]
                wacc += lax.dot_general(flat_scr[:, cut], wb, last, preferred_element_type=F32)
            if n > 0:
                old = tiles[n - 1]
                picked = jnp.concatenate([flat_scr[XH : XH + 32, old], flat_scr[QF:, old]], axis=0)
                acc += lax.dot_general(picked, c_scr[:, old], last, preferred_element_type=F32)
            if n < len(tiles):
                mis = chain(base, slot, cut, mis)
            if n == 0 and ahead > 1:
                row_block(i + 2, slot)
        scl += jnp.sum((bent * wacc).reshape(LANES // 8, 8, tm), axis=0)
        less = acc[0:32] - wacc[XH : XH + 32]
        pull = less[0:16] + less[16:32]
        wsum = wacc[ONE : ONE + 1]
        rate = acc[32 + ONE - QF : 33 + ONE - QF] - wsum
        for k in range(tm // 64):
            cut = slice(64 * k, 64 * k + 64)
            to = i * (tm // 64) + k
            for j in range(8):
                line = jnp.concatenate([pull[j : j + 1, cut], pull[j + 8 : j + 9, cut]], axis=1)
                out_ref[to, :, 128 * j : 128 * j + 128] = line
            out_ref[to, :, 1024:1152] = jnp.concatenate([rate[:, cut], wsum[:, cut]], axis=1)
        return mis, scl

    def two(k, carry):
        carry = block(2 * k, 0, *carry)
        return block(2 * k + 1, 1, *carry)

    row_block(0, 0)
    if steps > 1:
        row_block(1, 1)
    squares(0, slice(0, total))
    loops = max(0, (steps - 2) // 2)
    carry = (jnp.zeros((8, tn), F32), jnp.zeros((8, tm), F32))
    carry = lax.fori_loop(0, loops, two, carry)
    for i in range(2 * loops, steps):
        carry = block(i, i % 2, *carry, ahead=steps - 1 - i)
    mis, scl = carry
    mis = jnp.sum(jnp.sum(mis, axis=0, keepdims=True), axis=1, keepdims=True)
    scl = jnp.sum(jnp.sum(scl, axis=0, keepdims=True), axis=1, keepdims=True)
    at = lax.broadcasted_iota(jnp.int32, (1, 128), 1)
    line = jnp.where(at == 0, mis, jnp.where(at == 1, scl, 0.0))
    out_ref[:, :, 1152:1280] = jnp.broadcast_to(line[None], (out_ref.shape[0], 1, 128))


def finish_kernel(part_ref, crd_ref, new_ref):
    sums = jnp.sum(part_ref[...], axis=0)
    lines = [sums[:, 128 * k : 128 * k + 128] for k in range(9)]
    half = jnp.concatenate(lines[:8], axis=0)
    pull = jnp.concatenate([half[:, 0:64], half[:, 64:128]], axis=0)
    rate = lines[8][:, 0:64]
    wsum = lines[8][:, 64:128]
    crd = crd_ref[...]
    new_ref[...] = crd + (rate * crd - pull) / wsum


def stress_kernel(part_ref, out_ref):
    sums = jnp.sum(part_ref[...], axis=0)
    out_ref[...] = sums[:, 0:1] / sums[:, 1:2]


def column_moves(n_row, n_col, n_depth):
    moves = []
    for row in range(n_row):
        for at in range(n_col * n_depth):
            moves.append((row * n_col * n_depth + at, (at % n_row * n_col + row) * n_depth + at // n_row))
    return moves


def shards(embeddings, coords, pair_weight):
    rows, cols = pair_weight.shape
    points = embeddings.shape[1]
    group = rows // points
    n_row, n_z, n_core, n_depth = (lax.axis_size(a) for a in ("row", "z", "core", "depth"))
    likes = n_z * n_depth

    shard = (48, 128)
    packed = pl.pallas_call(
        pack_kernel,
        out_shape=(
            jax.ShapeDtypeStruct(shard, BF16),
            jax.ShapeDtypeStruct((likes,) + shard, BF16),
        ),
        name="pack",
    )(embeddings, coords)
    moves = column_moves(n_row, n_z * n_core, n_depth)
    moved = lax.ppermute(packed[0], ("row", "z", "core", "depth"), moves)
    own = lax.all_to_all(packed[1], ("z", "depth"), 0, 0, tiled=True)
    moved = pl.pallas_call(
        spread_kernel,
        out_shape=jax.ShapeDtypeStruct((n_row,) + shard, BF16),
        cost_estimate=pl.CostEstimate(flops=10**10, bytes_accessed=10**8, transcendentals=0),
        name="spread",
    )(moved)
    moved, own = lax.optimization_barrier((moved, own))
    oth = lax.ppermute(own, "core", [(0, 1), (1, 0)])
    t_cols = lax.all_to_all(moved, "row", 0, 0, tiled=True)

    vmem = pl.BlockSpec(memory_space=pltpu.VMEM)
    tm = 256
    parts = pl.pallas_call(
        pairs_kernel,
        in_specs=[
            vmem,
            vmem,
            vmem,
            pl.BlockSpec(memory_space=pltpu.HBM),
        ],
        out_specs=vmem,
        out_shape=jax.ShapeDtypeStruct((group, 1, 1280), F32),
        scratch_shapes=[
            pltpu.VMEM((rows, cols), BF16),
            pltpu.VMEM((LANES, cols), BF16),
            pltpu.VMEM((LANES, cols), BF16),
            pltpu.VMEM((LANES, cols), BF16),
            pltpu.VMEM((2, tm, LANES), BF16),
            pltpu.VMEM((2, LANES, tm), BF16),
            pltpu.VMEM((tm, cols), BF16),
            pltpu.VMEM((2, tm, cols), F32),
            pltpu.VMEM((2, tm, cols), F32),
            pltpu.SemaphoreType.DMA((rows // tm,)),
        ],
        compiler_params=pltpu.CompilerParams(vmem_limit_bytes=52 * 1024 * 1024),
        name="pairs",
    )(own, oth, t_cols, pair_weight)
    parts = lax.all_to_all(parts, ("z", "core", "depth"), 0, 0, tiled=True)
    shares = jnp.sum(parts[:, :, 1152:], axis=0, keepdims=True)
    shares = lax.all_to_all(jnp.broadcast_to(shares, (n_row, 1, 128)), "row", 0, 0, tiled=True)
    new_coords = pl.pallas_call(
        finish_kernel,
        out_shape=jax.ShapeDtypeStruct(coords.shape, F32),
        cost_estimate=pl.CostEstimate(flops=100000, bytes_accessed=200000, transcendentals=0),
        name="finish",
    )(parts, coords)
    stress = pl.pallas_call(
        stress_kernel,
        out_shape=jax.ShapeDtypeStruct((1, 1), F32),
        name="stress",
    )(shares)
    return (new_coords, stress[0, 0])


def solution(mesh):
    n_row, n_col, n_depth = (mesh.shape[a] for a in ("row", "col", "depth"))
    fine = jax.sharding.Mesh(
        mesh.devices.reshape(n_row, n_col // 2, 2, n_depth), ("row", "z", "core", "depth")
    )
    points = P(None, ("row", "z", "core", "depth"))
    return jax.shard_map(
        shards,
        mesh=fine,
        in_specs=(points, points, P("row", ("z", "core", "depth"))),
        out_specs=(points, P()),
        check_vma=False,
    )
```

```python
import jax
import jax.numpy as jnp
from jax import lax
from jax.experimental import pallas as pl
from jax.experimental.pallas import tpu as pltpu
from jax.sharding import PartitionSpec as P

F32 = jnp.float32
BF16 = jnp.bfloat16

EMB, XH, XL, XH2, QF, QX, ONE, LANES = 0, 64, 80, 96, 112, 115, 118, 128
TINY = 1e-30


def bilinear_form(kind):
    a = lax.broadcasted_iota(jnp.int32, (LANES, LANES), 0)
    b = lax.broadcasted_iota(jnp.int32, (LANES, LANES), 1)

    def band(first, count, shift):
        return (a >= first) & (a < first + count) & (b == a + shift)

    if kind == 0:
        cross = band(EMB, 64, 0)
        square, unit = QF, 1.0 / 64.0
    else:
        cross = band(XH, 16, 0) | band(XL, 16, XH2 - XL) | band(XH2, 16, XL - XH2)
        square, unit = QX, 1.0
    norms = band(square, 3, ONE - square) | band(ONE, 3, square - ONE)
    return jnp.where(cross, -2.0 * unit, jnp.where(norms, unit, 0.0)).astype(BF16)


def split3(value):
    hi = value.astype(BF16).astype(F32)
    mid = (value - hi).astype(BF16).astype(F32)
    low = (value - hi - mid).astype(BF16).astype(F32)
    return hi, mid, low


def pack_kernel(emb_ref, crd_ref, own_ref, out_ref):
    emb = emb_ref[...].astype(F32)
    crd = crd_ref[...]
    hi = crd.astype(BF16).astype(F32)
    feats = jnp.concatenate([emb, hi, crd - hi], axis=0)
    half = feats.shape[0] // 2
    mine = jnp.concatenate([feats[:half], feats[half:]], axis=1).astype(BF16)
    own_ref[...] = mine
    for k in range(out_ref.shape[0]):
        out_ref[k] = mine


def unpack(shards):
    top, low = [], []
    for sh in shards:
        sh = sh.astype(F32)
        top.append(sh[:, 0:64])
        low.append(sh[:, 64:128])
    feats = jnp.concatenate([jnp.concatenate(top, axis=1), jnp.concatenate(low, axis=1)], axis=0)
    emb, hi, low = feats[0:64], feats[XH : XH + 16], feats[XL : XL + 16]
    crd = hi + low
    squares = split3(jnp.sum(emb * emb, axis=0, keepdims=True))
    squares += split3(jnp.sum(crd * crd, axis=0, keepdims=True))
    at = lax.broadcasted_iota(jnp.int32, (16, feats.shape[1]), 0)
    tail = jnp.where((at >= ONE - QF) & (at < ONE - QF + 3), 1.0, 0.0)
    for k, sq in enumerate(squares):
        tail = jnp.where(at == k, sq, tail)
    return jnp.concatenate([feats, hi, tail], axis=0)


def spread_kernel(own_ref, out_ref):
    own = own_ref[...]
    for k in range(out_ref.shape[0]):
        out_ref[k] = own


def pairs_kernel(own_ref, oth_ref, col_ref, w_hbm, out_ref, w_ref, f_scr, x_scr, flat_scr, rows_scr, feat_scr, acc_scr, sum_scr, c_scr, f_tiles, x_tiles, sems):
    total_rows, total = w_ref.shape
    tm = c_scr.shape[0]
    tn = min(256, total)
    steps = total_rows // tm
    first = lax.axis_index("core") == 0

    def fetch(i):
        at = pl.ds(i * tm, tm)
        return pltpu.make_async_copy(w_hbm.at[at, :], w_ref.at[at, :], sems.at[i])

    for i in range(steps):
        fetch(i).start()
    last = (((1,), (1,)), ((), ()))
    form_f = bilinear_form(0)
    form_x = bilinear_form(1)
    for s in range(0, col_ref.shape[0], 4):
        some = unpack([col_ref[k] for k in range(s, min(s + 4, col_ref.shape[0]))]).astype(BF16)
        cut = slice(64 * s, 64 * s + some.shape[1])
        flat_scr[:, cut] = some
        f_scr[:, cut] = jnp.dot(form_f, some, preferred_element_type=F32).astype(BF16)
        x_scr[:, cut] = jnp.dot(form_x, some, preferred_element_type=F32).astype(BF16)

    def row_block(i, slot):
        shards = []
        for k in range(tm // 256):
            at = i * (tm // 128) + 2 * k
            own = [own_ref[at], own_ref[at + 1]]
            oth = [oth_ref[at], oth_ref[at + 1]]
            shards += [jnp.where(first, a, b) for a, b in zip(own, oth)]
            shards += [jnp.where(first, b, a) for a, b in zip(own, oth)]
        feats = unpack(shards)
        feat_scr[slot] = feats.astype(BF16)
        rows_scr[slot] = feats.T.astype(BF16)

    def squares(slot, cut):
        rows = rows_scr[slot]
        f_tiles[slot, :, cut] = jnp.dot(rows, f_scr[:, cut], preferred_element_type=F32)
        x_tiles[slot, :, cut] = jnp.dot(rows, x_scr[:, cut], preferred_element_type=F32)

    def chain(base, slot, cut, mis):
        for r in range(0, tm, 32):
            f2 = jnp.maximum(f_tiles[slot, r : r + 32, cut], TINY)
            x2 = jnp.maximum(x_tiles[slot, r : r + 32, cut], TINY)
            w = w_ref[pl.ds(pl.multiple_of(base + r, 32), 32), cut].astype(F32)
            dissim = f2 * lax.rsqrt(f2)
            inv = lax.rsqrt(x2)
            diff = dissim - x2 * inv
            c_scr[r : r + 32, cut] = (w * (dissim * jnp.minimum(inv, 1.0))).astype(BF16)
            miss = w * (diff * diff)
            mis += (miss[0:8] + miss[8:16]) + (miss[16:24] + miss[24:32])
        return mis

    tiles = [slice(start, start + tn) for start in range(0, total, tn)]

    def product(cut):
        picked = jnp.concatenate([flat_scr[XH : XH + 32, cut], flat_scr[QF:, cut]], axis=0)
        return lax.dot_general(picked, c_scr[:, cut], last, preferred_element_type=F32)

    def finish(i, slot):
        acc = acc_scr[slot] + product(tiles[-1])
        pull = acc[0:16] + acc[16:32]
        rate = acc[32 + ONE - QF : 33 + ONE - QF]
        wsum = sum_scr[slot, 0:1]
        for k in range(tm // 64):
            cut = slice(64 * k, 64 * k + 64)
            to = i * (tm // 64) + k
            for j in range(8):
                line = jnp.concatenate([pull[j : j + 1, cut], pull[j + 8 : j + 9, cut]], axis=1)
                out_ref[to, :, 128 * j : 128 * j + 128] = line
            out_ref[to, :, 1024:1152] = jnp.concatenate([rate[:, cut], wsum[:, cut]], axis=1)

    def block(i, slot, mis, scl, ahead=2):
        fetch(i).wait()
        bent = jnp.dot(form_f, feat_scr[slot], preferred_element_type=F32)
        base = i * tm
        acc = jnp.zeros((48, tm), F32)
        wacc = jnp.zeros((LANES, tm), F32)
        for n, cut in enumerate(tiles):
            if ahead > 0:
                squares(1 - slot, cut)
            wb = w_ref[pl.ds(pl.multiple_of(base, tm), tm), cut]
            wacc += lax.dot_general(flat_scr[:, cut], wb, last, preferred_element_type=F32)
            if n > 0:
                acc += product(tiles[n - 1])
            if n == len(tiles) - 1:
                scl += jnp.sum((bent * wacc).reshape(LANES // 8, 8, tm), axis=0)
                acc_scr[slot] = acc - jnp.concatenate([wacc[XH : XH + 32], wacc[QF:]], axis=0)
                sum_scr[slot] = jnp.broadcast_to(wacc[ONE : ONE + 1], (8, tm))
            if n == 0 and len(tiles) > 1:
                finish(jnp.maximum(i - 1, 0), 1 - slot)
            mis = chain(base, slot, cut, mis)
            if n == 0 and ahead > 1:
                row_block(i + 2, slot)
        if len(tiles) == 1:
            finish(i, slot)
        return mis, scl

    def two(k, carry):
        carry = block(2 * k, 0, *carry)
        return block(2 * k + 1, 1, *carry)

    acc_scr[...] = jnp.zeros_like(acc_scr)
    sum_scr[...] = jnp.zeros_like(sum_scr)
    c_scr[:, tiles[-1]] = jnp.zeros((tm, tn), BF16)
    row_block(0, 0)
    if steps > 1:
        row_block(1, 1)
    squares(0, slice(0, total))
    loops = max(0, (steps - 2) // 2)
    carry = (jnp.zeros((8, tn), F32), jnp.zeros((8, tm), F32))
    carry = lax.fori_loop(0, loops, two, carry)
    for i in range(2 * loops, steps):
        carry = block(i, i % 2, *carry, ahead=steps - 1 - i)
    mis, scl = carry
    if len(tiles) > 1:
        finish(steps - 1, (steps - 1) % 2)
    mis = jnp.sum(jnp.sum(mis, axis=0, keepdims=True), axis=1, keepdims=True)
    scl = jnp.sum(jnp.sum(scl, axis=0, keepdims=True), axis=1, keepdims=True)
    at = lax.broadcasted_iota(jnp.int32, (1, 128), 1)
    line = jnp.where(at == 0, mis, jnp.where(at == 1, scl, 0.0))
    out_ref[:, :, 1152:1280] = jnp.broadcast_to(line[None], (out_ref.shape[0], 1, 128))


def finish_kernel(part_ref, crd_ref, new_ref):
    sums = jnp.sum(part_ref[...], axis=0)
    lines = [sums[:, 128 * k : 128 * k + 128] for k in range(9)]
    half = jnp.concatenate(lines[:8], axis=0)
    pull = jnp.concatenate([half[:, 0:64], half[:, 64:128]], axis=0)
    rate = lines[8][:, 0:64]
    wsum = lines[8][:, 64:128]
    crd = crd_ref[...]
    new_ref[...] = crd + (rate * crd - pull) / wsum


def stress_kernel(part_ref, out_ref):
    sums = jnp.sum(part_ref[...], axis=0)
    out_ref[...] = sums[:, 0:1] / sums[:, 1:2]


def column_moves(n_row, n_col, n_depth):
    moves = []
    for row in range(n_row):
        for at in range(n_col * n_depth):
            moves.append((row * n_col * n_depth + at, (at % n_row * n_col + row) * n_depth + at // n_row))
    return moves


def shards(embeddings, coords, pair_weight):
    rows, cols = pair_weight.shape
    points = embeddings.shape[1]
    group = rows // points
    n_row, n_z, n_core, n_depth = (lax.axis_size(a) for a in ("row", "z", "core", "depth"))
    likes = n_z * n_depth

    shard = (48, 128)
    packed = pl.pallas_call(
        pack_kernel,
        out_shape=(
            jax.ShapeDtypeStruct(shard, BF16),
            jax.ShapeDtypeStruct((likes,) + shard, BF16),
        ),
        name="pack",
    )(embeddings, coords)
    moves = column_moves(n_row, n_z * n_core, n_depth)
    moved = lax.ppermute(packed[0], ("row", "z", "core", "depth"), moves)
    own = lax.all_to_all(packed[1], ("z", "depth"), 0, 0, tiled=True)
    moved = pl.pallas_call(
        spread_kernel,
        out_shape=jax.ShapeDtypeStruct((n_row,) + shard, BF16),
        cost_estimate=pl.CostEstimate(flops=10**10, bytes_accessed=10**8, transcendentals=0),
        name="spread",
    )(moved)
    moved, own = lax.optimization_barrier((moved, own))
    oth = lax.ppermute(own, "core", [(0, 1), (1, 0)])
    t_cols = lax.all_to_all(moved, "row", 0, 0, tiled=True)

    vmem = pl.BlockSpec(memory_space=pltpu.VMEM)
    tm = 256
    parts = pl.pallas_call(
        pairs_kernel,
        in_specs=[
            vmem,
            vmem,
            vmem,
            pl.BlockSpec(memory_space=pltpu.HBM),
        ],
        out_specs=vmem,
        out_shape=jax.ShapeDtypeStruct((group, 1, 1280), F32),
        scratch_shapes=[
            pltpu.VMEM((rows, cols), BF16),
            pltpu.VMEM((LANES, cols), BF16),
            pltpu.VMEM((LANES, cols), BF16),
            pltpu.VMEM((LANES, cols), BF16),
            pltpu.VMEM((2, tm, LANES), BF16),
            pltpu.VMEM((2, LANES, tm), BF16),
            pltpu.VMEM((2, 48, tm), F32),
            pltpu.VMEM((2, 8, tm), F32),
            pltpu.VMEM((tm, cols), BF16),
            pltpu.VMEM((2, tm, cols), F32),
            pltpu.VMEM((2, tm, cols), F32),
            pltpu.SemaphoreType.DMA((rows // tm,)),
        ],
        compiler_params=pltpu.CompilerParams(vmem_limit_bytes=52 * 1024 * 1024),
        name="pairs",
    )(own, oth, t_cols, pair_weight)
    parts = lax.all_to_all(parts, ("z", "core", "depth"), 0, 0, tiled=True)
    shares = jnp.sum(parts[:, :, 1152:], axis=0, keepdims=True)
    shares = lax.all_to_all(jnp.broadcast_to(shares, (n_row, 1, 128)), "row", 0, 0, tiled=True)
    new_coords = pl.pallas_call(
        finish_kernel,
        out_shape=jax.ShapeDtypeStruct(coords.shape, F32),
        cost_estimate=pl.CostEstimate(flops=100000, bytes_accessed=200000, transcendentals=0),
        name="finish",
    )(parts, coords)
    stress = pl.pallas_call(
        stress_kernel,
        out_shape=jax.ShapeDtypeStruct((1, 1), F32),
        name="stress",
    )(shares)
    return (new_coords, stress[0, 0])


def solution(mesh):
    n_row, n_col, n_depth = (mesh.shape[a] for a in ("row", "col", "depth"))
    fine = jax.sharding.Mesh(
        mesh.devices.reshape(n_row, n_col // 2, 2, n_depth), ("row", "z", "core", "depth")
    )
    points = P(None, ("row", "z", "core", "depth"))
    return jax.shard_map(
        shards,
        mesh=fine,
        in_specs=(points, points, P("row", ("z", "core", "depth"))),
        out_specs=(points, P()),
        check_vma=False,
    )
```
